256 devices in a mesh: seq: 64 (over z, y, core), head: 4 (over x).
Axes of the slice: x: 4, y: 4, z: 8, core: 2. Of those that a mesh axis runs over, the one named last changes fastest.
Arguments:
- hidden_in: bfloat16 [8192, 6144], P('seq', 'head'), may hold values from -60 to 60
- query_rows: bfloat16 [8192, 6144], P('seq', 'head'), may hold values from -6 to 6
- key_rows: bfloat16 [8192, 6144], P('seq', 'head'), may hold values from -6 to 6
- value_rows: bfloat16 [8192, 6144], P('seq', 'head'), may hold values from -6 to 6
- log_decay: float32 [8192, 48], P('seq', 'head'), may hold values from -1 to 0
- expert_ids: int32 [8192, 2], P('seq'), may hold values from 0 to 7, all different within a row; in each aligned block of 128 rows (0 to 127, 128 to 255, ...) at most 40 rows name the same one
- gate_values: float32 [8192, 2], P('seq'), may hold values from 0.2 to 1
- gate_weight: bfloat16 [6144, 36864], P('head', 'seq'), may hold values from -0.078125 to 0.078125
- up_weight: bfloat16 [6144, 36864], P('head', 'seq'), may hold values from -0.078125 to 0.078125
- down_weight: bfloat16 [36864, 6144], P('seq', 'head'), may hold values from -0.09375 to 0.09375
Outputs:
- attended: bfloat16 [8192, 6144], P('seq', 'head')
- mixed: bfloat16 [8192, 6144], P('seq', 'head')
The draws below stay inside these ranges and needn't reach their ends.
Inputs may be any that keep to these rules, and one draw needn't show every extreme that they name: `expert_ids`: each token names two different experts. The tokens of one index of seq name one expert at most 40 times, and some index of seq names some expert exactly 40 times.
All inputs are finite; a program needn't handle non-finite values.
Results may differ from the reference program's by a relative error of at most 0.0095.
Values may be sent and summed in bfloat16 or wider, within the bound.
A program may use at most 128 MiB of HBM per device.

```python
import math
import jax
import jax.numpy as jnp
import numpy as np
from jax import lax

DECAY_HEADS = 48
DH = 128
D = 6144
FF = 4608
EXPERTS = 8
TOK_DEV = 128
CAP = 40
SEQUENCE_TOKENS = 8192
N_SEQ = 64
N_HEAD = 4


def draw_hidden_in(key, part):
    key = jax.random.fold_in(key, 3)
    random_child_keys = jax.random.split(key, 3)
    noise_part = jnp.clip(jax.random.normal(random_child_keys[0], (SEQUENCE_TOKENS, D), jnp.float32), -4.0, 4.0)
    row_scale = jnp.exp(jax.random.uniform(random_child_keys[1], (SEQUENCE_TOKENS, 1), jnp.float32, jnp.log(0.3), jnp.log(3.0)))
    col_scale = jnp.exp(jax.random.uniform(random_child_keys[2], (1, D), jnp.float32, jnp.log(0.3), jnp.log(3.0)))
    col_place = jnp.arange(D).astype(jnp.float32)[None, :] / D
    rise_factor = jnp.power(3.0, 0.5 * col_place)
    return jnp.clip(noise_part * row_scale * col_scale * rise_factor, -60.0, 60.0).astype(jnp.bfloat16)


def draw_log_decay(key, part):
    key = jax.random.fold_in(key, 7)
    random_child_keys = jax.random.split(key, 7)
    slow_share = 0.5
    slow_heads = jax.random.uniform(random_child_keys[0], (DECAY_HEADS,), jnp.float32) < slow_share
    slow_rate = jnp.exp(jax.random.uniform(random_child_keys[1], (DECAY_HEADS,), jnp.float32, jnp.log(0.05), 0.0)) / SEQUENCE_TOKENS
    fast_rate = jnp.exp(jax.random.uniform(random_child_keys[2], (DECAY_HEADS,), jnp.float32, jnp.log(1.0 / 50.0), jnp.log(1.0 / 30.0)))
    baseline_decay_rate = jnp.where(slow_heads, slow_rate, fast_rate)
    block_count = SEQUENCE_TOKENS // TOK_DEV
    block_multiplier = jnp.exp(jax.random.uniform(random_child_keys[3], (block_count, DECAY_HEADS), jnp.float32, jnp.log(0.5), jnp.log(2.0)))
    block_multiplier = jnp.repeat(block_multiplier, TOK_DEV, axis=0)
    jitter_multiplier = jnp.exp(jax.random.uniform(random_child_keys[4], (SEQUENCE_TOKENS, DECAY_HEADS), jnp.float32, jnp.log(0.7), jnp.log(1.4)))
    spike_locations = jax.random.randint(random_child_keys[5], (2, DECAY_HEADS), 0, SEQUENCE_TOKENS)
    spike_length = jax.random.uniform(random_child_keys[6], (2, DECAY_HEADS), jnp.float32, 0.22, 0.5)
    token_offsets = jnp.arange(SEQUENCE_TOKENS)[:, None]
    decay_spikes = jnp.where(token_offsets == spike_locations[0][None, :], spike_length[0][None, :], 0.0)
    decay_spikes = decay_spikes + jnp.where(token_offsets == spike_locations[1][None, :], spike_length[1][None, :], 0.0)
    return -(baseline_decay_rate[None, :] * block_multiplier * jitter_multiplier) - decay_spikes


def shard_levels(key, shape, cuts, least, largest):
    loudness, own = 1.0, jax.random.fold_in(key, 6)
    for dim, blocks in cuts:
        draws = jnp.exp(jax.random.uniform(jax.random.fold_in(own, dim), (blocks,), jnp.float32, least / len(cuts), largest / len(cuts)))
        loudness = loudness * jnp.repeat(draws, shape[dim] // blocks).reshape([-1 if axis == dim else 1 for axis in range(len(shape))])
    return loudness


def shared_out(stream_key, own, number, rows, amount, top, reach, skew):
    order = jax.random.permutation(stream_key, amount)
    packed, common = portions_of(amount, rows * top, reach, skew, True), portions_of(amount, rows * top, reach, skew, False)
    places = jnp.arange(amount)

    def named(lengths, turn):
        used = int((lengths > 0).sum())
        fixed = max(1, used // 4)
        passed = fixed + (places - fixed + turn * (used - fixed)) % max(1, amount - fixed)
        return jnp.zeros((amount,), jnp.int32).at[order[jnp.where(places < fixed, places, passed)]].set(jnp.asarray(lengths, jnp.int32))

    lengths = jnp.where(number % 4 == 0, named(packed, number // 4), named(common, number - number // 4 - 1))
    mixed = jax.random.permutation(jax.random.fold_in(own, 3), amount)
    giver, sink = mixed[0:amount // 2 * 2:2], mixed[1:amount // 2 * 2:2]
    room = jnp.minimum(lengths[giver] - 1, reach - lengths[sink]) // 2
    room = jnp.where((giver == order[0]) | (sink == order[0]) | (lengths[sink] == 0), 0, jnp.maximum(room, 0))
    passed = jax.random.randint(jax.random.fold_in(own, 4), (amount // 2,), 0, 1 << 20) % (room + 1)
    lengths = lengths.at[giver].add(-passed).at[sink].add(passed)
    members = jnp.searchsorted(jnp.cumsum(lengths), jnp.arange(rows * top), side="right").astype(jnp.int32)
    listing = members.reshape(top, rows).T
    listing = listing[jax.random.permutation(jax.random.fold_in(own, 1), rows)]
    turn = jax.random.randint(jax.random.fold_in(own, 2), (rows, 1), 0, top)
    return jnp.take_along_axis(listing, (jnp.arange(top)[None, :] + turn) % top, axis=1)


def portions_of(amount, total, limit, skew, full):
    loads = [(1 << 20) // math.isqrt(grade ** skew) + 1 for grade in range(1, amount + 1)]
    largest = limit if full else min(limit, max(-(-total // amount), total * loads[0] // sum(loads)))
    least = 1 if total - largest >= amount - 1 else 0
    counts, rest = [largest] + [least] * (amount - 1), total - largest - least * (amount - 1)
    while rest > 0:
        candidates = [i for i in range(1, amount) if counts[i] < largest] or [i for i in range(1, amount) if counts[i] < limit]
        mass, remaining = sum([loads[i] for i in candidates]), rest
        for i in candidates:
            addition = min(limit - counts[i], max(1, remaining * loads[i] // mass), rest)
            counts[i] = counts[i] + addition
            rest = rest - addition
    return np.array(counts)


def normal_values(key, shape, scale, limit, pieces=(), kind=jnp.bfloat16):
    values = scale * jax.random.normal(key, shape, jnp.float32)
    if pieces:
        values = values * shard_levels(key, shape, pieces, -0.22, 0.18)
    return jnp.clip(values, -limit, limit).astype(kind)


def setup_inputs(seed: int = 0) -> dict:
    streams_of = jax.random.split(jax.random.key(seed), 11)
    hidden_in = draw_hidden_in(jax.random.fold_in(streams_of[10], 71), 0)
    query_rows = normal_values(streams_of[1], (SEQUENCE_TOKENS, D), 1.0, 6.0, ((0, 64), (1, 4)))
    key_rows = normal_values(streams_of[2], (SEQUENCE_TOKENS, D), 1.0, 6.0, ((0, 64), (1, 4)))
    value_rows = normal_values(streams_of[3], (SEQUENCE_TOKENS, D), 1.0, 6.0, ((0, 64), (1, 4)))
    log_decay = draw_log_decay(jax.random.fold_in(streams_of[10], 71), 0)
    expert_ids_keys = jax.random.split(jax.random.fold_in(streams_of[5], 1), SEQUENCE_TOKENS // TOK_DEV)
    expert_ids_turns = jax.random.permutation(jax.random.fold_in(streams_of[5], 3), SEQUENCE_TOKENS // TOK_DEV)
    expert_ids = jax.vmap(lambda own, number: shared_out(jax.random.fold_in(streams_of[5], 2), own, number, TOK_DEV, EXPERTS, 2, CAP, 2))(expert_ids_keys, expert_ids_turns).reshape((SEQUENCE_TOKENS, 2))
    gate_values = jnp.clip(0.2 + 0.8 * jax.random.uniform(streams_of[6], (SEQUENCE_TOKENS, 2), jnp.float32) ** shard_levels(streams_of[6], (SEQUENCE_TOKENS, 2), ((0, 64),), -0.2, 0.2), 0.2, 1.0)
    gate_weight = normal_values(streams_of[7], (D, EXPERTS * FF), D ** -0.5, 0.078125, ((0, 4), (1, 64)))
    up_weight = normal_values(streams_of[8], (D, EXPERTS * FF), D ** -0.5, 0.078125, ((0, 4), (1, 64)))
    down_weight = normal_values(streams_of[9], (EXPERTS * FF, D), FF ** -0.5, 0.09375, ((0, 64), (1, 4)))
    return dict(hidden_in=hidden_in, query_rows=query_rows, key_rows=key_rows, value_rows=value_rows, log_decay=log_decay, expert_ids=expert_ids, gate_values=gate_values, gate_weight=gate_weight, up_weight=up_weight, down_weight=down_weight)


def rounded(array):
    return lax.optimization_barrier(array.astype(jnp.bfloat16)).astype(jnp.float32)

def attend(hidden_in, query_rows, key_rows, value_rows, log_decay):
    scaling = DH ** (-0.5)
    token_offsets = jnp.arange(TOK_DEV)
    causal = (token_offsets[:, None] >= token_offsets[None, :])[:, :, None]

    def block_step(state, inputs):
        hidden_blk, query_blk, key_blk, value_blk, decay_blk = inputs
        query_f = query_blk.astype(jnp.float32)
        key_f = key_blk.astype(jnp.float32)
        value_f = value_blk.astype(jnp.float32)
        cumul = jnp.cumsum(decay_blk, axis=0)
        spread = jnp.where(causal, cumul[:, None, :] - cumul[None, :, :], 0.0)
        decay_mask = jnp.where(causal, jnp.exp(spread), 0.0)
        scores = jnp.einsum('thd,shd->hts', query_f, key_f) * scaling * jnp.transpose(decay_mask, (2, 0, 1))
        intra = jnp.einsum('hts,shd->thd', rounded(scores), value_f)
        query_decayed = rounded(query_f * (scaling * jnp.exp(cumul))[:, :, None])
        inter = jnp.einsum('thd,hde->the', query_decayed, rounded(state))
        block_total = cumul[-1]
        key_decayed = rounded(key_f * jnp.exp(block_total[None, :] - cumul)[:, :, None])
        local_state = jnp.einsum('shd,she->hde', key_decayed, value_f)
        new_state = jnp.exp(block_total)[:, None, None] * state + local_state
        mixed_heads = intra + inter
        normed = mixed_heads * lax.rsqrt(lax.optimization_barrier(jnp.mean(mixed_heads * mixed_heads, axis=2, keepdims=True)) + 1e-05)
        result = (hidden_blk.astype(jnp.float32) + normed.reshape(TOK_DEV, D)).astype(jnp.bfloat16)
        return (new_state, result)
    inputs = (hidden_in.reshape(N_SEQ, TOK_DEV, D), query_rows.reshape(N_SEQ, TOK_DEV, DECAY_HEADS, DH), key_rows.reshape(N_SEQ, TOK_DEV, DECAY_HEADS, DH), value_rows.reshape(N_SEQ, TOK_DEV, DECAY_HEADS, DH), log_decay.reshape(N_SEQ, TOK_DEV, DECAY_HEADS))
    start_state = jnp.zeros((DECAY_HEADS, DH, DH), jnp.float32)
    final_state, blocks = lax.scan(block_step, start_state, inputs)
    return blocks.reshape(SEQUENCE_TOKENS, D)

def mix_experts(attended, expert_ids, gate_values, gate_weight, up_weight, down_weight):
    group_size = N_SEQ // EXPERTS
    group_width = FF // group_size
    part_width = D // N_HEAD
    slot_total = N_SEQ * CAP
    attended_f = attended.astype(jnp.float32)
    mean_square = lax.optimization_barrier(jnp.mean(attended_f * attended_f, axis=1, keepdims=True))
    normed_rows = (attended_f * lax.rsqrt(mean_square + 1e-06)).astype(jnp.bfloat16)

    def head_sum(rows, weight):
        result = jnp.zeros((rows.shape[0], weight.shape[1]), jnp.float32)
        for head_index in range(N_HEAD):
            lower = head_index * part_width
            product = jnp.dot(rows[:, lower:lower + part_width], weight[lower:lower + part_width], preferred_element_type=jnp.float32)
            result = result + rounded(product)
        return result

    def add_expert(expert, mixture):
        expert = jnp.asarray(expert).astype(jnp.int32)
        chosen = expert_ids == expert
        picked = jnp.any(chosen, axis=1)
        order = jnp.argsort(jnp.where(picked, 0, 1).astype(jnp.int32), stable=True)[:slot_total]
        weighting = lax.optimization_barrier(jnp.sum(jnp.where(chosen, gate_values, 0.0), axis=1))[order]
        rows = normed_rows[order]
        start = (expert * FF).astype(jnp.int32)
        gate_cols = lax.dynamic_slice_in_dim(gate_weight, start, FF, 1)
        up_cols = lax.dynamic_slice_in_dim(up_weight, start, FF, 1)
        down_part = lax.dynamic_slice_in_dim(down_weight, start, FF, 0)
        pre_gate = head_sum(rows, gate_cols)
        pre_up = head_sum(rows, up_cols)
        activations = (jax.nn.silu(pre_gate) * pre_up).astype(jnp.bfloat16)
        result = jnp.zeros((slot_total, D), jnp.float32)
        for group_index in range(group_size):
            lower = group_index * group_width
            product = jnp.dot(activations[:, lower:lower + group_width], down_part[lower:lower + group_width], preferred_element_type=jnp.float32)
            result = result + rounded(product)
        return mixture.at[order].add(weighting[:, None] * result)
    mixture = lax.fori_loop(0, EXPERTS, add_expert, jnp.zeros((SEQUENCE_TOKENS, D), jnp.float32))
    return (attended_f + mixture).astype(jnp.bfloat16)

def reference(hidden_in, query_rows, key_rows, value_rows, log_decay, expert_ids, gate_values, gate_weight, up_weight, down_weight):
    attended = attend(hidden_in, query_rows, key_rows, value_rows, log_decay)
    mixed = mix_experts(attended, expert_ids, gate_values, gate_weight, up_weight, down_weight)
    return (attended, mixed)
```

```python
import jax
import jax.numpy as jnp
from jax import lax
from jax.experimental import pallas as pl
from jax.experimental.pallas import tpu as pltpu
from jax.sharding import PartitionSpec as P

MESH = pl.DeviceIdType.MESH
BF = jnp.bfloat16
F32 = jnp.float32

NZ, NY, NX = 8, 4, 4
NP = 8
T = 128
W = 1536
HW = 768
NH = 12
DH = 128
SL = NH * 16
CAP = 40
B = 2 * CAP
CH = 4 * B
NC = 8
FFD = 576
GU = 2 * FFD
AW = 640
SCALE = DH**-0.5
HALVES = ((0, 4, 3, 5), (1, 7, 2, 6))
PLACE = {dz: (h, k) for h, half in enumerate(HALVES) for k, dz in enumerate(half)}


def rcopy(src, dst, ss, rs, dev):
    return pltpu.make_async_remote_copy(
        src_ref=src, dst_ref=dst, send_sem=ss, recv_sem=rs, device_id=dev, device_id_type=MESH
    )


def dot(a, b, dims=((1,), (0,)), precision=None):
    return lax.dot_general(
        a, b, (dims, ((), ())), preferred_element_type=F32, precision=precision
    )


def kernel(
    hid, q, k, v, ld, meta, gw, uw, tw, dw,
    att, mix,
    s_loc, s_in, tot, tot_in, pfx, z_out, z_in, zt_out, zt_in, i_out, i_in,
    intra, qd, sq_out, sq_in, n_half, a_chip, meta_in, code, gate,
    packed, xb, wgu, wdn, acc, part, rs_in, act, d_send, d_keep, d_in, y_in, z_send, z_ret,
    m_out, m_in,
    e1s, e1r, t1s, t1r, e2s, e2r, t2s, t2r, e3s, e3r, sqs, sqr, hs, hr, ms, mr,
    zs, zr, ys, yr, bs, br, rss, rsr, ags, agr, ds, dr, fs, fr, zbs, zbr, os_, or_, wsem,
):
    s = lax.axis_index("seq")
    x = lax.axis_index("head")
    z = s // NP
    p = s % NP
    y = p // 2
    c = p % 2

    def plane(d):
        return (z * NP + (p + d) % NP, x)

    def zpeer(d):
        return (((z + d) % NZ) * NP + p, x)

    def ypeer(d):
        return (z * NP + ((y + d) % NY) * 2 + c, x)

    def xpeer(d):
        return (s, (x + d) % NX)

    sib = (z * NP + y * 2 + (1 - c), x)

    loads = []
    for h in range(2):
        rows = pl.ds(h * HW, HW)
        loads.append((gw.at[rows, pl.ds(0, 512)], wgu.at[h, :, pl.ds(0, 512)]))
        loads.append((uw.at[rows, pl.ds(0, 512)], wgu.at[h, :, pl.ds(512, 512)]))
        loads.append((tw.at[rows, :], wgu.at[h, :, pl.ds(1024, 128)]))
        loads.append((dw.at[:, pl.ds(h * HW, HW)], wdn.at[h, pl.ds(0, FFD), :]))
    loads = [pltpu.make_async_copy(a, b, wsem.at[i]) for i, (a, b) in enumerate(loads)]
    for copy in loads:
        copy.start()

    barrier = pltpu.get_barrier_semaphore()
    for d in range(1, NP):
        pl.semaphore_signal(barrier, inc=1, device_id=plane(d), device_id_type=MESH)
    for d in range(1, NZ):
        pl.semaphore_signal(barrier, inc=1, device_id=zpeer(d), device_id_type=MESH)
    for d in range(1, NX):
        pl.semaphore_signal(barrier, inc=1, device_id=xpeer(d), device_id_type=MESH)

    row = lax.broadcasted_iota(jnp.int32, (T, T), 0)
    col = lax.broadcasted_iota(jnp.int32, (T, T), 1)
    causal = row >= col
    hi = lax.Precision.HIGHEST
    lower = causal.astype(F32)
    upper = (row <= col).astype(F32)
    cumul = dot(lower, ld[...], precision=hi)
    cumul_t = dot(meta[...], upper, precision=hi)
    total = dot(meta[...], jnp.ones((T, T), F32), precision=hi)
    tot[...] = total
    for h in range(NH):
        hd = pl.ds(h * DH, DH)
        keyed = k[:, hd].astype(F32) * jnp.exp(total[h : h + 1, :] - cumul[:, h : h + 1])
        state = dot(keyed.astype(BF), v[:, hd], ((0,), (0,))).astype(BF)
        for j in range(NP):
            s_loc[j, pl.ds(16 * h, 16), :] = state[16 * j : 16 * j + 16, :]

    pl.semaphore_wait(barrier, (NP - 1) + (NZ - 1) + (NX - 1))

    meta_copy = rcopy(meta, meta_in, ms.at[0], mr.at[0], sib)
    meta_copy.start()

    def scan_one(d):
        return rcopy(s_loc.at[(p + d) % NP], s_in.at[p], e1s.at[d - 1], e1r.at[d - 1], plane(d))

    def scan_one_total(d):
        return rcopy(tot, tot_in.at[p], t1s.at[d - 1], t1r.at[d - 1], plane(d))

    for d in range(1, NP):
        scan_one_total(d).start()
        scan_one(d).start()
    s_in[p] = s_loc[p]
    tot_in[p] = tot[...]

    for h in range(NH):
        hd = pl.ds(h * DH, DH)
        own = cumul[:, h : h + 1]
        spread = jnp.where(causal, own - cumul_t[h : h + 1, :], 0.0)
        scores = dot(q[:, hd], k[:, hd], ((1,), (1,))) * SCALE
        weights = jnp.where(causal, scores * jnp.exp(spread), 0.0).astype(BF)
        intra[:, hd] = dot(weights, v[:, hd])
        qd[:, hd] = (q[:, hd].astype(F32) * (SCALE * jnp.exp(own))).astype(BF)

    for d in range(1, NP):
        scan_one_total(d).wait_recv()
        scan_one(d).wait_recv()

    def heads(tile):
        return jnp.concatenate(
            [jnp.broadcast_to(tile[h : h + 1, :], (16, DH)) for h in range(NH)], axis=0
        )

    run = jnp.zeros((SL, DH), F32)
    for j in range(NP):
        pfx[j] = run
        run = heads(jnp.exp(tot_in[j])) * run + s_in[j].astype(F32)
    z_out[...] = run.astype(BF)
    zt_out[...] = sum(tot_in[j] for j in range(NP))

    def scan_two(d):
        return rcopy(z_out, z_in.at[z], e2s.at[d - 1], e2r.at[d - 1], zpeer(d))

    def scan_two_total(d):
        return rcopy(zt_out, zt_in.at[z], t2s.at[d - 1], t2r.at[d - 1], zpeer(d))

    for d in range(1, NZ):
        scan_two_total(d).start()
        scan_two(d).start()
    z_in[z] = z_out[...]
    zt_in[z] = zt_out[...]

    meta_copy.wait_recv()
    expert = lax.broadcasted_iota(jnp.int32, (8, T), 0).astype(F32)
    strict = (row < col).astype(BF)

    def routing(m):
        first, second = expert == m[12:13, :], expert == m[13:14, :]
        chosen = jnp.where(first, 1.0, 0.0) + jnp.where(second, 1.0, 0.0)
        rank = dot(chosen.astype(BF), strict)
        value = jnp.where(first, m[14:15, :], 0.0) + jnp.where(second, m[15:16, :], 0.0)
        return jnp.where(chosen > 0.5, rank, -1000.0), value

    rank, value = routing(meta[...])
    mine = pl.ds(pl.multiple_of(c * T, T), T)
    code[:, mine] = rank + (c * CAP).astype(F32)
    gate[:, mine] = value
    rank, value = routing(meta_in[...])
    other = pl.ds(pl.multiple_of((1 - c) * T, T), T)
    code[:, other] = rank + ((1 - c) * CAP).astype(F32)
    gate[:, other] = value

    for d in range(1, NZ):
        scan_two_total(d).wait_recv()
        scan_two(d).wait_recv()
    run = jnp.zeros((SL, DH), F32)
    for j in range(NZ):
        new = heads(jnp.exp(zt_in[j])) * run + z_in[j].astype(F32)
        run = jnp.where(j < z, new, run)

    def scan_three(d):
        return rcopy(i_out.at[(p + d) % NP], i_in.at[p], e3s.at[d - 1], e3r.at[d - 1], plane(d))

    before = jnp.zeros((16, DH), F32)
    for j in range(NP):
        i_out[j] = (pfx[j] + heads(jnp.exp(before)) * run).astype(BF)
        before = before + tot_in[j]
    for d in range(1, NP):
        scan_three(d).start()
    i_in[p] = i_out[p]
    for d in range(1, NP):
        scan_three(d).wait_recv()

    squares = jnp.zeros((T, DH), F32)
    for h in range(NH):
        hd = pl.ds(h * DH, DH)
        state = jnp.concatenate([i_in[j, pl.ds(16 * h, 16), :] for j in range(NP)], axis=0)
        o = intra[:, hd] + dot(qd[:, hd], state)
        o = o * lax.rsqrt(jnp.mean(o * o, axis=1, keepdims=True) + 1e-05)
        a = (hid[:, hd].astype(F32) + o).astype(BF)
        att[:, hd] = a
        a = a.astype(F32)
        squares = squares + a * a
    sq_out[...] = squares

    def square(d):
        return rcopy(sq_out, sq_in.at[d - 1], sqs.at[d - 1], sqr.at[d - 1], xpeer(d))

    for d in range(1, NX):
        square(d).start()
    for d in range(1, NX):
        square(d).wait_recv()
        squares = squares + sq_in[d - 1]
    scale = lax.rsqrt(jnp.sum(squares, axis=1, keepdims=True) / (W * NX) + 1e-06)
    for h in range(2):
        n_half[h] = (att[:, pl.ds(h * HW, HW)].astype(F32) * scale).astype(BF)

    half_copy = rcopy(n_half.at[1 - c], a_chip.at[c], hs.at[0], hr.at[0], sib)
    half_copy.start()
    a_chip[c] = n_half[c]
    for copy in loads:
        copy.wait()
    for h in range(2):
        wdn[h, pl.ds(FFD, AW - FFD), :] = jnp.zeros((AW - FFD, HW), BF)
    half_copy.wait_recv()

    slot = lax.broadcasted_iota(jnp.int32, (B, 2 * T), 0).astype(F32)

    def dispatch(d):
        half, at = PLACE[(NZ - d) % NZ]
        return rcopy(
            packed.at[d], xb.at[c, 7 * half, pl.ds(B * at, B), :], zs.at[d - 1], zr.at[d - 1], zpeer(d)
        )

    tokens = a_chip[...].reshape(2 * T, HW)
    for d in (4, 5, 3, 7, 1, 6, 2, 0):
        e = (z + d) % NZ
        pick = (slot == code[pl.ds(e, 1), :]).astype(BF)
        rows = dot(pick, tokens).astype(BF)
        if d:
            packed[d] = rows
            dispatch(d).start()
        else:
            xb[c, 0, pl.ds(0, B), :] = rows

    def spread_y(half, d):
        at = NY - d if half == 0 else 4 + (3 - d)
        return rcopy(
            xb.at[c, 7 * half], xb.at[c, at], ys.at[half, d - 1], yr.at[at - 1], ypeer(d)
        )

    def arrive(half):
        for dz in HALVES[half]:
            if dz:
                dispatch(NZ - dz).wait_recv()
        for d in (1, 3, 2):
            spread_y(half, d).start()

    def landed_y(t):
        return rcopy(xb.at[c, t], xb.at[c, t], ys.at[0, 0], yr.at[t - 1], ypeer(1))

    def spread_core(t):
        return rcopy(xb.at[c, t], xb.at[c, t], bs.at[t], br.at[t], sib)

    def landed_core(t):
        return rcopy(xb.at[1 - c, t], xb.at[1 - c, t], bs.at[t], br.at[t], sib)

    def reduce_x(t, d):
        return rcopy(
            part.at[t, (x + d) % NX], rs_in.at[t, d - 1], rss.at[t, d - 1], rsr.at[t, d - 1], xpeer(d)
        )

    def gather_x(t, d):
        mine = act.at[t, x]
        return rcopy(mine, mine, ags.at[t, d - 1], agr.at[t, d - 1], xpeer(d))

    def landed_x(t, d):
        there = act.at[t, (x + NX - d) % NX]
        return rcopy(there, there, ags.at[t, d - 1], agr.at[t, d - 1], xpeer(d))

    def pair_down(t):
        return rcopy(d_send.at[t], d_in.at[t], ds.at[t], dr.at[t], sib)

    def return_y(t):
        dy = (t + t // 4) % NY
        half = t // 4
        return rcopy(
            d_keep.at[t], y_in.at[half, 3 - dy], fs.at[t], fr.at[half, 3 - dy], ypeer(dy)
        )

    def landed_return(half, i):
        return rcopy(y_in.at[half, i], y_in.at[half, i], fs.at[1], fr.at[half, i], ypeer(1))

    def return_z(dz):
        half, at = PLACE[dz]
        return rcopy(
            z_send.at[half, at], z_ret.at[(NZ - dz) % NZ], zbs.at[dz - 1], zbr.at[dz - 1], zpeer(dz)
        )

    def finish(half):
        for i in range(3):
            landed_return(half, i).wait_recv()
        for at, dz in enumerate(HALVES[half]):
            rows = pl.ds(B * at, B)
            whole = d_keep[7 * half, rows, :].astype(F32)
            for i in range(3):
                whole = whole + y_in[half, i, rows, :].astype(F32)
            if dz:
                z_send[half, at] = whole.astype(BF)
                return_z(dz).start()
            else:
                z_ret[0] = whole.astype(BF)

    cuts = [(n, min(256, GU - n)) for n in range(0, GU, 256)]

    def step(t, carry):
        @pl.when(t == 0)
        def _():
            arrive(0)

        @pl.when(t < NC)
        def _():
            @pl.when((t > 0) & (t < NC - 1))
            def _():
                landed_y(t).wait_recv()

            spread_core(t).start()
            for n, w in cuts:
                acc[:, pl.ds(n, w)] = dot(xb[c, t], wgu[c, :, pl.ds(n, w)])
            landed_core(t).wait_recv()
            for n, w in cuts:
                out = acc[:, pl.ds(n, w)] + dot(xb[1 - c, t], wgu[1 - c, :, pl.ds(n, w)])
                out = out.astype(BF)
                for i in range(NX):
                    part[t, i, :, pl.ds(n, w)] = out[B * i : B * i + B, :]
            for d in (2, 1, 3):
                reduce_x(t, d).start()

        @pl.when(t == 0)
        def _():
            arrive(1)

        @pl.when((t >= 1) & (t < NC + 1))
        def _():
            u = t - 1
            for d in range(1, NX):
                reduce_x(u, d).wait_recv()

            def whole(n, w):
                lanes = pl.ds(n, w)
                out = part[u, x, :, lanes].astype(F32)
                for i in range(NX - 1):
                    out = out + rs_in[u, i, :, lanes].astype(F32)
                return out

            g, up = whole(0, 512), whole(512, 512)
            act[u, x, :, pl.ds(0, 512)] = (g / (1.0 + jnp.exp(-g)) * up).astype(BF)
            g = whole(1024, 128)
            up = pltpu.roll(g, 64, 1)
            lane = lax.broadcasted_iota(jnp.int32, (B, 128), 1)
            both = g / (1.0 + jnp.exp(-g)) * up
            act[u, x, :, pl.ds(512, 128)] = jnp.where(lane < 64, both, 0.0).astype(BF)
            for d in (2, 1, 3):
                gather_x(u, d).start()

        @pl.when((t >= 2) & (t < NC + 2))
        def _():
            u = t - 2
            for d in range(1, NX):
                landed_x(u, d).wait_recv()
            a = act[u].reshape(CH, AW)
            for n in range(0, HW, 256):
                d_send[u, :, pl.ds(n, 256)] = dot(a, wdn[1 - c, :, pl.ds(n, 256)]).astype(BF)
            pair_down(u).start()
            for n in range(0, HW, 256):
                d_keep[u, :, pl.ds(n, 256)] = dot(a, wdn[c, :, pl.ds(n, 256)]).astype(BF)
            pair_down(u).wait_recv()
            d_keep[u] = (d_keep[u].astype(F32) + d_in[u].astype(F32)).astype(BF)

            @pl.when((u > 0) & (u < NC - 1))
            def _():
                return_y(u).start()

        @pl.when(t == NC)
        def _():
            finish(0)

        return carry

    lax.fori_loop(0, NC + 2, step, 0)
    finish(1)

    for d in range(1, NZ):
        return_z(d).wait_recv()
    total = jnp.zeros((2 * T, HW), F32)
    for d in range(NZ):
        e = (z + d) % NZ
        pick = jnp.where(slot == code[pl.ds(e, 1), :], gate[pl.ds(e, 1), :], 0.0)
        high = pick.astype(BF)
        low = (pick - high.astype(F32)).astype(BF)
        rows = z_ret[d]
        total = total + dot(high, rows, ((0,), (0,))) + dot(low, rows, ((0,), (0,)))
    m_out[0] = total[:T]
    m_out[1] = total[T:]
    mix_copy = rcopy(m_out.at[1 - c], m_in, os_.at[0], or_.at[0], sib)
    mix_copy.start()
    lanes = pl.ds(pl.multiple_of(c * HW, HW), HW)
    mix[:, lanes] = (att[:, lanes].astype(F32) + m_out[c]).astype(BF)
    mix_copy.wait_recv()
    lanes = pl.ds(pl.multiple_of((1 - c) * HW, HW), HW)
    mix[:, lanes] = (att[:, lanes].astype(F32) + m_in[...]).astype(BF)

    meta_copy.wait_send()
    half_copy.wait_send()
    mix_copy.wait_send()
    for d in range(1, NP):
        scan_one(d).wait_send()
        scan_one_total(d).wait_send()
        scan_three(d).wait_send()
    for d in range(1, NZ):
        scan_two(d).wait_send()
        scan_two_total(d).wait_send()
        dispatch(d).wait_send()
        return_z(d).wait_send()
    for d in range(1, NX):
        square(d).wait_send()
        for half in range(2):
            spread_y(half, d).wait_send()

    def sent(t, carry):
        spread_core(t).wait_send()
        pair_down(t).wait_send()
        for d in range(1, NX):
            reduce_x(t, d).wait_send()
            gather_x(t, d).wait_send()

        @pl.when((t > 0) & (t < NC - 1))
        def _():
            return_y(t).wait_send()

        return carry

    lax.fori_loop(0, NC, sent, 0)


def on_device(hid, q, k, v, ld, ids, gates, gw, uw, dw):
    meta = jnp.concatenate([ld.T, ids.T.astype(F32), gates.T], axis=0)
    tail = jnp.concatenate([gw[:, 512:], uw[:, 512:]], axis=1)
    vmem = pl.BlockSpec(memory_space=pltpu.VMEM)
    anywhere = pl.BlockSpec(memory_space=pl.ANY)
    sem = pltpu.SemaphoreType.DMA
    buffers = [
        ((NP, SL, DH), BF), ((NP, SL, DH), BF), ((16, DH), F32), ((NP, 16, DH), F32),
        ((NP, SL, DH), F32), ((SL, DH), BF), ((NZ, SL, DH), BF), ((16, DH), F32),
        ((NZ, 16, DH), F32), ((NP, SL, DH), BF), ((NP, SL, DH), BF),
        ((T, W), F32), ((T, W), BF), ((T, DH), F32), ((NX - 1, T, DH), F32),
        ((2, T, HW), BF), ((2, T, HW), BF), ((16, T), F32), ((8, 2 * T), F32), ((8, 2 * T), F32),
        ((NZ, B, HW), BF), ((2, NC, CH, HW), BF), ((2, HW, GU), BF), ((2, AW, HW), BF),
        ((CH, GU), F32), ((NC, NX, B, GU), BF), ((NC, NX - 1, B, GU), BF),
        ((NC, NX, B, AW), BF), ((NC, CH, HW), BF), ((NC, CH, HW), BF), ((NC, CH, HW), BF),
        ((2, NY - 1, CH, HW), BF), ((2, 4, B, HW), BF), ((NZ, B, HW), BF),
        ((2, T, HW), F32), ((T, HW), F32),
    ]
    pairs = [
        (7,), (7,), (7,), (7,), (7,), (3,), (1,), (1,),
    ]
    sems = [sem(n) for n in pairs for _ in range(2)]
    sems += [sem((7,)), sem((7,)), sem((2, 3)), sem((6,)), sem((NC,)), sem((NC,))]
    sems += [sem((NC, 3)), sem((NC, 3)), sem((NC, 3)), sem((NC, 3)), sem((NC,)), sem((NC,))]
    sems += [sem((NC,)), sem((2, 3)), sem((7,)), sem((7,)), sem((1,)), sem((1,)), sem((8,))]
    return pl.pallas_call(
        kernel,
        out_shape=(jax.ShapeDtypeStruct((T, W), BF), jax.ShapeDtypeStruct((T, W), BF)),
        in_specs=[vmem] * 6 + [anywhere] * 4,
        out_specs=(vmem, vmem),
        scratch_shapes=[pltpu.VMEM(shape, kind) for shape, kind in buffers] + sems,
        compiler_params=pltpu.CompilerParams(
            collective_id=0, has_side_effects=True, vmem_limit_bytes=60 << 20
        ),
        name="layer",
    )(hid, q, k, v, ld, meta, gw, uw, tail, dw)


def solution(mesh):
    placed = (
        P("seq", "head"),
        P("seq", "head"),
        P("seq", "head"),
        P("seq", "head"),
        P("seq", "head"),
        P("seq", None),
        P("seq", None),
        P("head", "seq"),
        P("head", "seq"),
        P("seq", "head"),
    )
    return jax.shard_map(
        on_device,
        mesh=mesh,
        in_specs=placed,
        out_specs=(P("seq", "head"), P("seq", "head")),
        check_vma=False,
    )
```

```python
import jax
import jax.numpy as jnp
from jax import lax
from jax.experimental import pallas as pl
from jax.experimental.pallas import tpu as pltpu
from jax.sharding import PartitionSpec as P

MESH = pl.DeviceIdType.MESH
BF = jnp.bfloat16
F32 = jnp.float32

NZ, NY, NX = 8, 4, 4
NP = 8
T = 128
W = 1536
HW = 768
NH = 12
DH = 128
SL = NH * 16
CAP = 40
B = 2 * CAP
CH = NY * B
NC = NZ
FFD = 576
GU = 2 * FFD
AW = 640
SCALE = DH**-0.5
DZ = (0, 1, 6, 2, 5, 3, 4, 7)


def rcopy(src, dst, ss, rs, dev):
    return pltpu.make_async_remote_copy(
        src_ref=src, dst_ref=dst, send_sem=ss, recv_sem=rs, device_id=dev, device_id_type=MESH
    )


def dot(a, b, dims=((1,), (0,)), precision=None):
    return lax.dot_general(
        a, b, (dims, ((), ())), preferred_element_type=F32, precision=precision
    )


def kernel(
    hid, q, k, v, ldt, idt, gt, gw, uw, dw,
    att, mix,
    s_loc, s_in, tot, tot_in, pfx, z_out, z_in, zt_out, zt_in, i_out, i_in,
    intra, qd, sq_out, sq_in, n_half, a_chip, tokens, meta, meta_in, code, gate,
    packed, xb, wgu, wdn, part, rs_in, act, d_send, d_keep, d_in, y_in, z_send, z_ret,
    m_out, m_in,
    e1s, e1r, t1s, t1r, e2s, e2r, t2s, t2r, e3s, e3r, sqs, sqr, hs, hr, ms, mr,
    zs, zr, ys, yr, bs, br, rss, rsr, ags, agr, ds, dr, fs, fr, zbs, zbr, os_, or_, wsem,
):
    s = lax.axis_index("seq")
    x = lax.axis_index("head")
    z = s // NP
    p = s % NP
    y = p // 2
    c = p % 2

    def plane(d):
        return (z * NP + (p + d) % NP, x)

    def zpeer(d):
        return (((z + d) % NZ) * NP + p, x)

    def ypeer(d):
        return (z * NP + ((y + d) % NY) * 2 + c, x)

    def xpeer(d):
        return (s, (x + d) % NX)

    def xcore(dc, dx):
        return (z * NP + y * 2 + (c + dc) % 2, (x + dx) % NX)

    sib = (z * NP + y * 2 + (1 - c), x)

    loads = []
    for h in range(2):
        half = pl.ds(h * HW, HW)
        loads.append((gw.at[pl.ds(0, 512), half], wgu.at[h, pl.ds(0, 512), :]))
        loads.append((uw.at[pl.ds(0, 512), half], wgu.at[h, pl.ds(512, 512), :]))
        loads.append((gw.at[pl.ds(512, 64), half], wgu.at[h, pl.ds(1024, 64), :]))
        loads.append((uw.at[pl.ds(512, 64), half], wgu.at[h, pl.ds(1088, 64), :]))
        loads.append((dw.at[:, half], wdn.at[h, pl.ds(0, FFD), :]))
    loads = [pltpu.make_async_copy(a, b, wsem.at[i]) for i, (a, b) in enumerate(loads)]
    for copy in loads:
        copy.start()

    barrier = pltpu.get_barrier_semaphore()
    for d in range(1, NP):
        pl.semaphore_signal(barrier, inc=1, device_id=plane(d), device_id_type=MESH)
    for d in range(1, NZ):
        pl.semaphore_signal(barrier, inc=1, device_id=zpeer(d), device_id_type=MESH)
    for d in range(1, NX):
        pl.semaphore_signal(barrier, inc=1, device_id=xpeer(d), device_id_type=MESH)
        pl.semaphore_signal(barrier, inc=1, device_id=xcore(1, d), device_id_type=MESH)

    row = lax.broadcasted_iota(jnp.int32, (T, T), 0)
    col = lax.broadcasted_iota(jnp.int32, (T, T), 1)
    causal = row >= col
    hi = lax.Precision.HIGHEST
    lower = causal.astype(F32)
    upper = (row <= col).astype(F32)
    meta[pl.ds(0, NH), :] = ldt[...]
    meta[pl.ds(NH, 2), :] = idt[...].astype(F32)
    meta[pl.ds(NH + 2, 2), :] = gt[...]
    cumul = dot(lower, meta[...], ((1,), (1,)), precision=hi)
    cumul_t = dot(meta[...], upper, precision=hi)
    total = dot(meta[...], jnp.ones((T, T), F32), precision=hi)
    tot[...] = total
    for h in range(NH):
        hd = pl.ds(h * DH, DH)
        keyed = k[:, hd].astype(F32) * jnp.exp(total[h : h + 1, :] - cumul[:, h : h + 1])
        state = dot(keyed.astype(BF), v[:, hd], ((0,), (0,))).astype(BF)
        for j in range(NP):
            s_loc[j, pl.ds(16 * h, 16), :] = state[16 * j : 16 * j + 16, :]

    pl.semaphore_wait(barrier, (NP - 1) + (NZ - 1) + 2 * (NX - 1))

    meta_copy = rcopy(meta, meta_in, ms.at[0], mr.at[0], sib)
    meta_copy.start()

    def scan_one(d):
        return rcopy(s_loc.at[(p + d) % NP], s_in.at[p], e1s.at[d - 1], e1r.at[d - 1], plane(d))

    def scan_one_total(d):
        return rcopy(tot, tot_in.at[p], t1s.at[d - 1], t1r.at[d - 1], plane(d))

    for d in range(1, NP):
        scan_one_total(d).start()
        scan_one(d).start()
    s_in[p] = s_loc[p]
    tot_in[p] = tot[...]

    for h in range(NH):
        hd = pl.ds(h * DH, DH)
        own = cumul[:, h : h + 1]
        spread = jnp.where(causal, own - cumul_t[h : h + 1, :], 0.0)
        scores = dot(q[:, hd], k[:, hd], ((1,), (1,))) * SCALE
        weights = jnp.where(causal, scores * jnp.exp(spread), 0.0).astype(BF)
        intra[:, hd] = dot(weights, v[:, hd])
        qd[:, hd] = (q[:, hd].astype(F32) * (SCALE * jnp.exp(own))).astype(BF)

    for d in range(1, NP):
        scan_one_total(d).wait_recv()
        scan_one(d).wait_recv()

    def heads(tile):
        return jnp.concatenate(
            [jnp.broadcast_to(tile[h : h + 1, :], (16, DH)) for h in range(NH)], axis=0
        )

    run = jnp.zeros((SL, DH), F32)
    for j in range(NP):
        pfx[j] = run
        run = heads(jnp.exp(tot_in[j])) * run + s_in[j].astype(F32)
    z_out[...] = run.astype(BF)
    zt_out[...] = sum(tot_in[j] for j in range(NP))

    def scan_two(d):
        return rcopy(z_out, z_in.at[z], e2s.at[d - 1], e2r.at[d - 1], zpeer(d))

    def scan_two_total(d):
        return rcopy(zt_out, zt_in.at[z], t2s.at[d - 1], t2r.at[d - 1], zpeer(d))

    for d in range(1, NZ):
        scan_two_total(d).start()
        scan_two(d).start()
    z_in[z] = z_out[...]
    zt_in[z] = zt_out[...]

    meta_copy.wait_recv()
    expert = lax.broadcasted_iota(jnp.int32, (8, T), 0).astype(F32)
    strict = (row < col).astype(BF)

    def routing(m):
        first, second = expert == m[12:13, :], expert == m[13:14, :]
        chosen = jnp.where(first, 1.0, 0.0) + jnp.where(second, 1.0, 0.0)
        rank = dot(chosen.astype(BF), strict)
        value = jnp.where(first, m[14:15, :], 0.0) + jnp.where(second, m[15:16, :], 0.0)
        return jnp.where(chosen > 0.5, rank, -1000.0), value

    rank, value = routing(meta[...])
    mine = pl.ds(pl.multiple_of(c * T, T), T)
    code[:, mine] = rank + (c * CAP).astype(F32)
    gate[:, mine] = value
    rank, value = routing(meta_in[...])
    other = pl.ds(pl.multiple_of((1 - c) * T, T), T)
    code[:, other] = rank + ((1 - c) * CAP).astype(F32)
    gate[:, other] = value

    for d in range(1, NZ):
        scan_two_total(d).wait_recv()
        scan_two(d).wait_recv()
    run = jnp.zeros((SL, DH), F32)
    for j in range(NZ):
        new = heads(jnp.exp(zt_in[j])) * run + z_in[j].astype(F32)
        run = jnp.where(j < z, new, run)

    def scan_three(d):
        return rcopy(i_out.at[(p + d) % NP], i_in.at[p], e3s.at[d - 1], e3r.at[d - 1], plane(d))

    before = jnp.zeros((16, DH), F32)
    for j in range(NP):
        i_out[j] = (pfx[j] + heads(jnp.exp(before)) * run).astype(BF)
        before = before + tot_in[j]
    for d in range(1, NP):
        scan_three(d).start()
    i_in[p] = i_out[p]
    for d in range(1, NP):
        scan_three(d).wait_recv()

    squares = jnp.zeros((T, DH), F32)
    for h in range(NH):
        hd = pl.ds(h * DH, DH)
        state = jnp.concatenate([i_in[j, pl.ds(16 * h, 16), :] for j in range(NP)], axis=0)
        o = intra[:, hd] + dot(qd[:, hd], state)
        o = o * lax.rsqrt(jnp.mean(o * o, axis=1, keepdims=True) + 1e-05)
        a = (hid[:, hd].astype(F32) + o).astype(BF)
        att[:, hd] = a
        n_half[h // 6, :, pl.ds(DH * (h % 6), DH)] = a
        a = a.astype(F32)
        squares = squares + a * a
    half_copy = rcopy(n_half.at[1 - c], a_chip, hs.at[0], hr.at[0], sib)
    half_copy.start()

    sq_out[...] = dot(jnp.ones((8, T), F32), squares, ((1,), (1,)), precision=hi)
    others = [(dc, dx) for dc in range(2) for dx in range(NX) if dc or dx]

    def square(dc, dx):
        i = NX * dc + dx - 1
        return rcopy(sq_out, sq_in.at[c, x], sqs.at[i], sqr.at[i], xcore(dc, dx))

    for dc, dx in others:
        square(dc, dx).start()
    sq_in[c, x] = sq_out[...]
    for dc, dx in others:
        square(dc, dx).wait_recv()

    def normed(core, rows):
        whole = sum(sq_in[core, i] for i in range(NX))
        scale = lax.rsqrt(whole / (W * NX) + 1e-06).T[:, 0:1]
        return (rows.astype(F32) * scale).astype(BF)

    tokens[c] = normed(c, n_half[c])
    for h in range(2):
        wdn[h, pl.ds(FFD, AW - FFD), :] = jnp.zeros((AW - FFD, HW), BF)
    half_copy.wait_recv()
    tokens[1 - c] = normed(1 - c, a_chip[...])

    slot = lax.broadcasted_iota(jnp.int32, (B, 2 * T), 0).astype(F32)

    def dispatch(t):
        return rcopy(packed.at[t], xb.at[c, t, 0], zs.at[t], zr.at[t], zpeer(NZ - DZ[t]))

    def distance(t):
        return (1 - t % 2) * ((7 - t // 2) % 7) + (t % 2) * (1 + t // 2 + 3 * (t // 7))

    def landed_z(t):
        return rcopy(xb.at[c, t, 0], xb.at[c, t, 0], zs.at[t], zr.at[t], zpeer(1))

    def along(t):
        return 1 + 2 * (t % 2)

    def spread_y(t, d):
        return rcopy(
            xb.at[c, t, 0], xb.at[c, t, NY - d], ys.at[t, d - 1], yr.at[t, d - 1], ypeer(d)
        )

    def relay_y(t):
        d = along(t)
        return rcopy(xb.at[c, t, NY - d], xb.at[c, t, 2], ys.at[t, 1], yr.at[t, 1], ypeer(d))

    def pass_y(t):
        spread_y(t, along(t)).wait_recv()
        relay_y(t).start()

    def take_z(t):
        landed_z(t).wait_recv()
        spread_y(t, 1).start()
        spread_y(t, 3).start()

    def spread_core(t):
        return rcopy(xb.at[c, t], xb.at[c, t], bs.at[t], br.at[t], sib)

    def landed_core(t):
        return rcopy(xb.at[1 - c, t], xb.at[1 - c, t], bs.at[t], br.at[t], sib)

    def pass_core(t):
        spread_y(t, NY - along(t)).wait_recv()
        relay_y(t).wait_recv()
        spread_core(t).start()

    def reduce_far(t):
        d = along(t)
        return rcopy(part.at[t, (x + 2) % NX], rs_in.at[t, 0], rss.at[t, 0], rsr.at[t, 0], xpeer(d))

    def reduce_near(t):
        d = NX - along(t)
        return rcopy(part.at[t, (x + d) % NX], rs_in.at[t, 1], rss.at[t, 1], rsr.at[t, 1], xpeer(d))

    def reduce_both(t):
        d = along(t)
        return rcopy(part.at[t, (x + d) % NX], rs_in.at[t, 2], rss.at[t, 2], rsr.at[t, 2], xpeer(d))

    def gather_x(t, d):
        mine = act.at[t, x]
        return rcopy(mine, mine, ags.at[t, d - 1], agr.at[t, d - 1], xpeer(d))

    def relay_x(t):
        d = along(t)
        there = act.at[t, (x + NX - d) % NX]
        return rcopy(there, there, ags.at[t, 1], agr.at[t, 1], xpeer(d))

    def pair_down(t):
        return rcopy(d_send.at[t], d_in.at[t], ds.at[t], dr.at[t], sib)

    def return_far(t):
        return rcopy(d_keep.at[t, 2], y_in.at[t, 0], fs.at[t, 0], fr.at[t, 0], ypeer(along(t)))

    def return_near(t):
        d = NY - along(t)
        return rcopy(d_keep.at[t, d], y_in.at[t, 1], fs.at[t, 1], fr.at[t, 1], ypeer(d))

    def return_both(t):
        d = along(t)
        return rcopy(d_keep.at[t, d], y_in.at[t, 2], fs.at[t, 2], fr.at[t, 2], ypeer(d))

    def return_z(t):
        return rcopy(z_send.at[t], z_ret.at[t], zbs.at[t], zbr.at[t], zpeer(distance(t)))

    chip = tokens[...].reshape(2 * T, HW)
    for t in range(NC):
        e = (z + NZ - DZ[t]) % NZ
        pick = (slot == code[pl.ds(e, 1), :]).astype(BF)
        rows = dot(pick, chip).astype(BF)
        if t:
            packed[t] = rows
            dispatch(t).start()
        else:
            xb[c, 0, 0] = rows
            spread_y(0, 1).start()
            spread_y(0, 3).start()
    for copy in loads:
        copy.wait()
    pass_y(0)
    take_z(1)
    pass_core(0)

    cuts = [(n, min(256, GU - n)) for n in range(0, GU, 256)]

    def expand(t):
        landed_core(t).wait_recv()
        own, other = xb[c, t].reshape(CH, HW), xb[1 - c, t].reshape(CH, HW)
        for n, w in cuts:
            out = dot(own, wgu[c, pl.ds(n, w), :], ((1,), (1,)))
            out = out + dot(other, wgu[1 - c, pl.ds(n, w), :], ((1,), (1,)))
            out = out.astype(BF)
            for i in range(NX):
                part[t, i, :, pl.ds(n, w)] = out[B * i : B * i + B, :]
        reduce_far(t).start()
        reduce_near(t).start()

    def reduce(u):
        reduce_far(u).wait_recv()
        there = (x + along(u)) % NX
        both = part[u, there].astype(F32) + rs_in[u, 0].astype(F32)
        part[u, there] = both.astype(BF)
        reduce_both(u).start()

    def activate(u):
        reduce_near(u).wait_recv()
        reduce_both(u).wait_recv()

        def whole(n, w):
            lanes = pl.ds(n, w)
            out = part[u, x, :, lanes].astype(F32)
            for i in (1, 2):
                out = out + rs_in[u, i, :, lanes].astype(F32)
            return out

        g, up = whole(0, 512), whole(512, 512)
        act[u, x, :, pl.ds(0, 512)] = (g / (1.0 + jnp.exp(-g)) * up).astype(BF)
        g = whole(1024, 128)
        up = pltpu.roll(g, 64, 1)
        lane = lax.broadcasted_iota(jnp.int32, (B, 128), 1)
        both = g / (1.0 + jnp.exp(-g)) * up
        act[u, x, :, pl.ds(512, 128)] = jnp.where(lane < 64, both, 0.0).astype(BF)
        gather_x(u, 1).start()
        gather_x(u, 3).start()

    def relay_act(u):
        gather_x(u, along(u)).wait_recv()
        relay_x(u).start()

    def project(u):
        gather_x(u, NX - along(u)).wait_recv()
        relay_x(u).wait_recv()
        a = act[u].reshape(CH, AW)
        for n in range(0, HW, 256):
            out = dot(a, wdn[1 - c, :, pl.ds(n, 256)]).astype(BF)
            d_send[u, :, :, pl.ds(n, 256)] = out.reshape(NY, B, 256)
        pair_down(u).start()
        for n in range(0, HW, 256):
            out = dot(a, wdn[c, :, pl.ds(n, 256)]).astype(BF)
            d_keep[u, :, :, pl.ds(n, 256)] = out.reshape(NY, B, 256)

    def pair(u):
        pair_down(u).wait_recv()
        for i in range(NY):
            both = d_keep[u, i].astype(F32) + d_in[u, i].astype(F32)
            d_keep[u, i] = both.astype(BF)
        return_far(u).start()
        return_near(u).start()

    def fold(u):
        return_far(u).wait_recv()
        d = along(u)
        both = d_keep[u, d].astype(F32) + y_in[u, 0].astype(F32)
        d_keep[u, d] = both.astype(BF)
        return_both(u).start()

    def give(u):
        return_near(u).wait_recv()
        return_both(u).wait_recv()
        whole = d_keep[u, 0].astype(F32)
        for i in (1, 2):
            whole = whole + y_in[u, i].astype(F32)
        whole = whole.astype(BF)

        @pl.when(u == 0)
        def _():
            z_ret[0] = whole

        @pl.when(u > 0)
        def _():
            z_send[u] = whole
            return_z(u).start()

    stages = [
        (give, 7, 0), (fold, 6, 0), (pair, 5, 0), (project, 4, 0), (relay_act, 3, 0), (activate, 2, 0),
        (reduce, 1, 0), (expand, 0, 0), (pass_core, -1, 1), (pass_y, -2, 1), (take_z, -3, 2),
    ]

    def step(t, carry):
        for stage, lag, first in stages:

            @pl.when((t - lag >= first) & (t - lag < NC))
            def _(stage=stage, lag=lag):
                stage(t - lag)

        return carry

    start = min(lag + first for _, lag, first in stages)
    lax.fori_loop(start, NC + max(lag for _, lag, _ in stages), step, 0)

    total = jnp.zeros((2 * T, HW), F32)
    for t in range(NC):
        if t:
            return_z(t).wait_recv()
        e = (z + NZ - DZ[t]) % NZ
        pick = jnp.where(slot == code[pl.ds(e, 1), :], gate[pl.ds(e, 1), :], 0.0)
        high = pick.astype(BF)
        low = (pick - high.astype(F32)).astype(BF)
        rows = z_ret[t]
        total = total + dot(high, rows, ((0,), (0,))) + dot(low, rows, ((0,), (0,)))
    m_out[0] = total[:T]
    m_out[1] = total[T:]
    mix_copy = rcopy(m_out.at[1 - c], m_in, os_.at[0], or_.at[0], sib)
    mix_copy.start()
    lanes = pl.ds(pl.multiple_of(c * HW, HW), HW)
    mix[:, lanes] = (att[:, lanes].astype(F32) + m_out[c]).astype(BF)
    mix_copy.wait_recv()
    lanes = pl.ds(pl.multiple_of((1 - c) * HW, HW), HW)
    mix[:, lanes] = (att[:, lanes].astype(F32) + m_in[...]).astype(BF)

    meta_copy.wait_send()
    half_copy.wait_send()
    mix_copy.wait_send()
    for d in range(1, NP):
        scan_one(d).wait_send()
        scan_one_total(d).wait_send()
        scan_three(d).wait_send()
    for d in range(1, NZ):
        scan_two(d).wait_send()
        scan_two_total(d).wait_send()
    for dc, dx in others:
        square(dc, dx).wait_send()

    def sent(t, carry):
        spread_y(t, 1).wait_send()
        spread_y(t, 3).wait_send()
        relay_y(t).wait_send()
        spread_core(t).wait_send()
        reduce_far(t).wait_send()
        reduce_near(t).wait_send()
        reduce_both(t).wait_send()
        gather_x(t, 1).wait_send()
        gather_x(t, 3).wait_send()
        relay_x(t).wait_send()
        pair_down(t).wait_send()
        return_far(t).wait_send()
        return_near(t).wait_send()
        return_both(t).wait_send()

        @pl.when(t > 0)
        def _():
            landed_z(t).wait_send()
            return_z(t).wait_send()

        return carry

    lax.fori_loop(0, NC, sent, 0)


def hand_over(a, b, a_out, b_out):
    a_out[...] = a[...]
    b_out[...] = b[...]


def on_device(hid, q, k, v, ld, ids, gates, gw, uw, dw):
    vmem = pl.BlockSpec(memory_space=pltpu.VMEM)
    anywhere = pl.BlockSpec(memory_space=pl.ANY)
    sem = pltpu.SemaphoreType.DMA
    buffers = [
        ((NP, SL, DH), BF), ((NP, SL, DH), BF), ((16, DH), F32), ((NP, 16, DH), F32),
        ((NP, SL, DH), F32), ((SL, DH), BF), ((NZ, SL, DH), BF), ((16, DH), F32),
        ((NZ, 16, DH), F32), ((NP, SL, DH), BF), ((NP, SL, DH), BF),
        ((T, W), F32), ((T, W), BF), ((8, T), F32), ((2, NX, 8, T), F32),
        ((2, T, HW), BF), ((T, HW), BF), ((2, T, HW), BF), ((16, T), F32), ((16, T), F32), ((8, 2 * T), F32), ((8, 2 * T), F32),
        ((NZ, B, HW), BF), ((2, NC, NY, B, HW), BF), ((2, GU, HW), BF), ((2, AW, HW), BF),
        ((NC, NX, B, GU), BF), ((NC, NX - 1, B, GU), BF),
        ((NC, NX, B, AW), BF), ((NC, NY, B, HW), BF), ((NC, NY, B, HW), BF), ((NC, NY, B, HW), BF),
        ((NC, 3, B, HW), BF), ((NC, B, HW), BF), ((NC, B, HW), BF),
        ((2, T, HW), F32), ((T, HW), F32),
    ]
    pairs = [
        (7,), (7,), (7,), (7,), (7,), (7,), (1,), (1,),
    ]
    sems = [sem(n) for n in pairs for _ in range(2)]
    three, one = sem((NC, 3)), sem((NC,))
    sems += [one, one, three, three, one, one, three, three, three, three, one, one, three, three]
    sems += [one, one, sem((1,)), sem((1,)), sem((10,))]
    shapes = (jax.ShapeDtypeStruct((T, W), BF), jax.ShapeDtypeStruct((T, W), BF))
    results = pl.pallas_call(
        kernel,
        out_shape=shapes,
        in_specs=[vmem] * 7 + [anywhere] * 3,
        out_specs=(vmem, vmem),
        scratch_shapes=[pltpu.VMEM(shape, kind) for shape, kind in buffers] + sems,
        compiler_params=pltpu.CompilerParams(
            collective_id=0, has_side_effects=True, vmem_limit_bytes=60 << 20
        ),
        name="layer",
    )(hid, q, k, v, ld.T, ids.T, gates.T, gw.T, uw.T, dw)
    return pl.pallas_call(
        hand_over,
        out_shape=shapes,
        in_specs=[vmem] * 2,
        out_specs=(vmem, vmem),
        name="results",
    )(*results)


def solution(mesh):
    placed = (
        P("seq", "head"),
        P("seq", "head"),
        P("seq", "head"),
        P("seq", "head"),
        P("seq", "head"),
        P("seq", None),
        P("seq", None),
        P("head", "seq"),
        P("head", "seq"),
        P("seq", "head"),
    )
    return jax.shard_map(
        on_device,
        mesh=mesh,
        in_specs=placed,
        out_specs=(P("seq", "head"), P("seq", "head")),
        check_vma=False,
    )
```

```python
import jax
import jax.numpy as jnp
from jax import lax
from jax.experimental import pallas as pl
from jax.experimental.pallas import tpu as pltpu
from jax.sharding import PartitionSpec as P

MESH = pl.DeviceIdType.MESH
BF = jnp.bfloat16
F32 = jnp.float32

NZ, NY, NX = 8, 4, 4
NP = 8
T = 128
W = 1536
HW = 768
NH = 12
DH = 128
SL = NH * 16
CAP = 40
B = 2 * CAP
CH = NY * B
NC = NZ
FFD = 576
GU = 2 * FFD
AW = 640
SCALE = DH**-0.5
SUM_WAYS = ((0, 640), (640, 512))
ACT_WAYS = ((384, 256), (0, 384))
ROW_WAYS = ((0, 384), (384, 384))
DZ = (0, 1, 6, 2, 5, 3, 4, 7)


def rcopy(src, dst, ss, rs, dev):
    return pltpu.make_async_remote_copy(
        src_ref=src, dst_ref=dst, send_sem=ss, recv_sem=rs, device_id=dev, device_id_type=MESH
    )


def dot(a, b, dims=((1,), (0,)), precision=None):
    return lax.dot_general(
        a, b, (dims, ((), ())), preferred_element_type=F32, precision=precision
    )


def kernel(
    hid, q, k, v, ldt, idt, gt, gw, uw, dw,
    att, mix,
    s_loc, s_in, tot, tot_in, pfx, z_out, z_in, zt_out, zt_in, i_out, i_in,
    intra, qd, sq_out, sq_in, n_half, a_chip, tokens, picks, meta, meta_in, code, gate,
    packed, xb, wgu, wdn, part, rs_in, act, d_send, d_keep, d_in, y_in, z_send, z_ret,
    m_out, m_in,
    e1s, e1r, t1s, t1r, e2s, e2r, t2s, t2r, e3s, e3r, sqs, sqr, hs, hr, ms, mr,
    zs, zr, ys, yr, bs, br, rss, rsr, ags, agr, ds, dr, fs, fr, zbs, zbr, os_, or_, wsem,
):
    s = lax.axis_index("seq")
    x = lax.axis_index("head")
    z = s // NP
    p = s % NP
    y = p // 2
    c = p % 2

    def plane(d):
        return (z * NP + (p + d) % NP, x)

    def zpeer(d):
        return (((z + d) % NZ) * NP + p, x)

    def ypeer(d):
        return (z * NP + ((y + d) % NY) * 2 + c, x)

    def xpeer(d):
        return (s, (x + d) % NX)

    def xcore(dc, dx):
        return (z * NP + y * 2 + (c + dc) % 2, (x + dx) % NX)

    sib = (z * NP + y * 2 + (1 - c), x)

    loads = []
    for h in range(2):
        half = pl.ds(h * HW, HW)
        loads.append((gw.at[pl.ds(0, 512), half], wgu.at[h, pl.ds(0, 512), :]))
        loads.append((uw.at[pl.ds(0, 512), half], wgu.at[h, pl.ds(512, 512), :]))
        loads.append((gw.at[pl.ds(512, 64), half], wgu.at[h, pl.ds(1024, 64), :]))
        loads.append((uw.at[pl.ds(512, 64), half], wgu.at[h, pl.ds(1088, 64), :]))
        loads.append((dw.at[:, half], wdn.at[h, pl.ds(0, FFD), :]))
    loads = [pltpu.make_async_copy(a, b, wsem.at[i]) for i, (a, b) in enumerate(loads)]
    for copy in loads:
        copy.start()

    barrier = pltpu.get_barrier_semaphore()
    for d in range(1, NP):
        pl.semaphore_signal(barrier, inc=1, device_id=plane(d), device_id_type=MESH)
    for d in range(1, NZ):
        pl.semaphore_signal(barrier, inc=1, device_id=zpeer(d), device_id_type=MESH)
    for d in range(1, NX):
        pl.semaphore_signal(barrier, inc=1, device_id=xpeer(d), device_id_type=MESH)
        pl.semaphore_signal(barrier, inc=1, device_id=xcore(1, d), device_id_type=MESH)

    row = lax.broadcasted_iota(jnp.int32, (T, T), 0)
    col = lax.broadcasted_iota(jnp.int32, (T, T), 1)
    causal = row >= col
    hi = lax.Precision.HIGHEST
    lower = causal.astype(F32)
    upper = (row <= col).astype(F32)
    meta[pl.ds(0, NH), :] = ldt[...]
    meta[pl.ds(NH, 2), :] = idt[...].astype(F32)
    meta[pl.ds(NH + 2, 2), :] = gt[...]
    cumul = dot(lower, meta[...], ((1,), (1,)), precision=hi)
    cumul_t = dot(meta[...], upper, precision=hi)
    total = dot(meta[...], jnp.ones((T, T), F32), precision=hi)
    tot[...] = total
    for h in range(NH):
        hd = pl.ds(h * DH, DH)
        keyed = k[:, hd].astype(F32) * jnp.exp(total[h : h + 1, :] - cumul[:, h : h + 1])
        state = dot(keyed.astype(BF), v[:, hd], ((0,), (0,))).astype(BF)
        for j in range(NP):
            s_loc[j, pl.ds(16 * h, 16), :] = state[16 * j : 16 * j + 16, :]

    pl.semaphore_wait(barrier, (NP - 1) + (NZ - 1) + 2 * (NX - 1))

    meta_copy = rcopy(meta, meta_in, ms.at[0], mr.at[0], sib)
    meta_copy.start()

    def scan_one(d):
        return rcopy(s_loc.at[(p + d) % NP], s_in.at[p], e1s.at[d - 1], e1r.at[d - 1], plane(d))

    def scan_one_total(d):
        return rcopy(tot, tot_in.at[p], t1s.at[d - 1], t1r.at[d - 1], plane(d))

    for d in range(1, NP):
        scan_one_total(d).start()
        scan_one(d).start()
    s_in[p] = s_loc[p]
    tot_in[p] = tot[...]

    for h in range(NH):
        hd = pl.ds(h * DH, DH)
        own = cumul[:, h : h + 1]
        spread = jnp.where(causal, own - cumul_t[h : h + 1, :], 0.0)
        scores = dot(q[:, hd], k[:, hd], ((1,), (1,))) * SCALE
        weights = jnp.where(causal, scores * jnp.exp(spread), 0.0).astype(BF)
        intra[:, hd] = dot(weights, v[:, hd])
        qd[:, hd] = (q[:, hd].astype(F32) * (SCALE * jnp.exp(own))).astype(BF)

    for d in range(1, NP):
        scan_one_total(d).wait_recv()
        scan_one(d).wait_recv()

    def heads(tile):
        return jnp.concatenate(
            [jnp.broadcast_to(tile[h : h + 1, :], (16, DH)) for h in range(NH)], axis=0
        )

    run = jnp.zeros((SL, DH), F32)
    for j in range(NP):
        pfx[j] = run
        run = heads(jnp.exp(tot_in[j])) * run + s_in[j].astype(F32)
    z_out[...] = run.astype(BF)
    zt_out[...] = sum(tot_in[j] for j in range(NP))

    def scan_two(d):
        return rcopy(z_out, z_in.at[z], e2s.at[d - 1], e2r.at[d - 1], zpeer(d))

    def scan_two_total(d):
        return rcopy(zt_out, zt_in.at[z], t2s.at[d - 1], t2r.at[d - 1], zpeer(d))

    for d in range(1, NZ):
        scan_two_total(d).start()
        scan_two(d).start()
    z_in[z] = z_out[...]
    zt_in[z] = zt_out[...]

    meta_copy.wait_recv()
    expert = lax.broadcasted_iota(jnp.int32, (8, T), 0).astype(F32)
    strict = (row < col).astype(BF)

    def routing(m):
        first, second = expert == m[12:13, :], expert == m[13:14, :]
        chosen = jnp.where(first, 1.0, 0.0) + jnp.where(second, 1.0, 0.0)
        rank = dot(chosen.astype(BF), strict)
        value = jnp.where(first, m[14:15, :], 0.0) + jnp.where(second, m[15:16, :], 0.0)
        return jnp.where(chosen > 0.5, rank, -1000.0), value

    rank, value = routing(meta[...])
    mine = pl.ds(pl.multiple_of(c * T, T), T)
    code[:, mine] = rank + (c * CAP).astype(F32)
    gate[:, mine] = value
    rank, value = routing(meta_in[...])
    other = pl.ds(pl.multiple_of((1 - c) * T, T), T)
    code[:, other] = rank + ((1 - c) * CAP).astype(F32)
    gate[:, other] = value

    slot = lax.broadcasted_iota(jnp.int32, (B, 2 * T), 0).astype(F32)
    for t in range(NC):
        e = (z + NZ - DZ[t]) % NZ
        picks[t] = (slot == code[pl.ds(e, 1), :]).astype(BF)
    for h in range(2):
        wdn[h, pl.ds(FFD, AW - FFD), :] = jnp.zeros((AW - FFD, HW), BF)

    for d in range(1, NZ):
        scan_two_total(d).wait_recv()
        scan_two(d).wait_recv()
    run = jnp.zeros((SL, DH), F32)
    for j in range(NZ):
        new = heads(jnp.exp(zt_in[j])) * run + z_in[j].astype(F32)
        run = jnp.where(j < z, new, run)

    def scan_three(d):
        return rcopy(i_out.at[(p + d) % NP], i_in.at[p], e3s.at[d - 1], e3r.at[d - 1], plane(d))

    before = jnp.zeros((16, DH), F32)
    for j in range(NP):
        i_out[j] = (pfx[j] + heads(jnp.exp(before)) * run).astype(BF)
        before = before + tot_in[j]
    for d in range(1, NP):
        scan_three(d).start()
    i_in[p] = i_out[p]
    for d in range(1, NP):
        scan_three(d).wait_recv()

    squares = jnp.zeros((T, DH), F32)
    for h in range(NH):
        hd = pl.ds(h * DH, DH)
        state = jnp.concatenate([i_in[j, pl.ds(16 * h, 16), :] for j in range(NP)], axis=0)
        o = intra[:, hd] + dot(qd[:, hd], state)
        o = o * lax.rsqrt(jnp.mean(o * o, axis=1, keepdims=True) + 1e-05)
        a = (hid[:, hd].astype(F32) + o).astype(BF)
        att[:, hd] = a
        n_half[h // 6, :, pl.ds(DH * (h % 6), DH)] = a
        a = a.astype(F32)
        squares = squares + a * a
    half_copy = rcopy(n_half.at[1 - c], a_chip, hs.at[0], hr.at[0], sib)
    half_copy.start()

    sq_out[...] = dot(jnp.ones((8, T), F32), squares, ((1,), (1,)), precision=hi)
    others = [(dc, dx) for dc in range(2) for dx in range(NX) if dc or dx]

    def square(dc, dx):
        i = NX * dc + dx - 1
        return rcopy(sq_out, sq_in.at[c, x], sqs.at[i], sqr.at[i], xcore(dc, dx))

    for dc, dx in others:
        square(dc, dx).start()
    sq_in[c, x] = sq_out[...]
    for dc, dx in others:
        square(dc, dx).wait_recv()

    def normed(core, rows):
        whole = sum(sq_in[core, i] for i in range(NX))
        scale = lax.rsqrt(whole / (W * NX) + 1e-06).T[:, 0:1]
        return (rows.astype(F32) * scale).astype(BF)

    tokens[c] = normed(c, n_half[c])
    half_copy.wait_recv()
    tokens[1 - c] = normed(1 - c, a_chip[...])

    def dispatch(t):
        return rcopy(packed.at[t], xb.at[c, t, 0], zs.at[t], zr.at[t], zpeer(NZ - DZ[t]))

    def distance(t):
        return (1 - t % 2) * ((7 - t // 2) % 7) + (t % 2) * (1 + t // 2 + 3 * (t // 7))

    def landed_z(t):
        return rcopy(xb.at[c, t, 0], xb.at[c, t, 0], zs.at[t], zr.at[t], zpeer(1))

    def spread_y(t, d):
        i = d // 2
        return rcopy(xb.at[c, t, 0], xb.at[c, t, NY - d], ys.at[t, i], yr.at[t, i], ypeer(d))

    def relay_y(t, way):
        d, lanes = 1 + 2 * way, pl.ds(*ROW_WAYS[way])
        return rcopy(
            xb.at[c, t, NY - d, :, lanes], xb.at[c, t, 2, :, lanes],
            ys.at[t, 2 + way], yr.at[t, 2 + way], ypeer(d),
        )

    def pass_y(t):
        for way in range(2):
            spread_y(t, 1 + 2 * way).wait_recv()
            relay_y(t, way).start()

    def take_z(t):
        landed_z(t).wait_recv()
        spread_y(t, 1).start()
        spread_y(t, 3).start()

    def spread_core(t):
        return rcopy(xb.at[c, t], xb.at[c, t], bs.at[t], br.at[t], sib)

    def landed_core(t):
        return rcopy(xb.at[1 - c, t], xb.at[1 - c, t], bs.at[t], br.at[t], sib)

    def pass_core(t):
        for way in range(2):
            relay_y(t, way).wait_recv()
        spread_core(t).start()

    def sum_x(t, way, d, at, kind):
        lanes = pl.ds(*SUM_WAYS[way])
        i = 2 * kind + way
        return rcopy(
            part.at[t, at, :, lanes], rs_in.at[t, kind, :, lanes], rss.at[t, i], rsr.at[t, i], xpeer(d)
        )

    def reduce_far(t, way):
        return sum_x(t, way, 1 + 2 * way, (x + 2) % NX, 0)

    def reduce_near(t, way):
        return sum_x(t, way, 3 - 2 * way, (x + 3 - 2 * way) % NX, 1)

    def reduce_both(t, way):
        return sum_x(t, way, 1 + 2 * way, (x + 1 + 2 * way) % NX, 2)

    def gather_x(t, d):
        mine = act.at[t, x]
        return rcopy(mine, mine, ags.at[t, d // 2], agr.at[t, d // 2], xpeer(d))

    def relay_x(t, way):
        d = 1 + 2 * way
        there = act.at[t, (x + NX - d) % NX, :, pl.ds(*ACT_WAYS[way])]
        return rcopy(there, there, ags.at[t, 2 + way], agr.at[t, 2 + way], xpeer(d))

    def pair_down(t):
        return rcopy(d_send.at[t], d_in.at[t], ds.at[t], dr.at[t], sib)

    def sum_y(t, way, d, at, kind):
        lanes = pl.ds(*ROW_WAYS[way])
        i = 2 * kind + way
        return rcopy(
            d_keep.at[t, at, :, lanes], y_in.at[t, kind, :, lanes], fs.at[t, i], fr.at[t, i], ypeer(d)
        )

    def return_far(t, way):
        return sum_y(t, way, 1 + 2 * way, 2, 0)

    def return_near(t, way):
        return sum_y(t, way, 3 - 2 * way, 3 - 2 * way, 1)

    def return_both(t, way):
        return sum_y(t, way, 1 + 2 * way, 1 + 2 * way, 2)

    def return_z(t):
        return rcopy(z_send.at[t], z_ret.at[t], zbs.at[t], zbr.at[t], zpeer(distance(t)))

    chip = tokens[...].reshape(2 * T, HW)
    for t in range(NC):
        rows = dot(picks[t], chip).astype(BF)
        if t:
            packed[t] = rows
            dispatch(t).start()
        else:
            xb[c, 0, 0] = rows
            spread_y(0, 1).start()
            spread_y(0, 3).start()
    for copy in loads:
        copy.wait()
    pass_y(0)
    take_z(1)
    pass_core(0)

    cuts = [(n, min(256, GU - n)) for n in range(0, GU, 256)]

    def expand(t):
        landed_core(t).wait_recv()
        own, other = xb[c, t].reshape(CH, HW), xb[1 - c, t].reshape(CH, HW)
        for n, w in cuts:
            out = dot(own, wgu[c, pl.ds(n, w), :], ((1,), (1,)))
            out = out + dot(other, wgu[1 - c, pl.ds(n, w), :], ((1,), (1,)))
            out = out.astype(BF)
            for i in range(NX):
                part[t, i, :, pl.ds(n, w)] = out[B * i : B * i + B, :]
        for way in range(2):
            reduce_far(t, way).start()
        for way in range(2):
            reduce_near(t, way).start()

    def reduce(u):
        for way in range(2):
            there, lanes = (x + 1 + 2 * way) % NX, pl.ds(*SUM_WAYS[way])
            reduce_far(u, way).wait_recv()
            both = part[u, there, :, lanes].astype(F32) + rs_in[u, 0, :, lanes].astype(F32)
            part[u, there, :, lanes] = both.astype(BF)
            reduce_both(u, way).start()

    def activate(u):
        for way in range(2):
            reduce_near(u, way).wait_recv()
            reduce_both(u, way).wait_recv()

        def whole(n, w):
            lanes = pl.ds(n, w)
            out = part[u, x, :, lanes].astype(F32)
            for i in (1, 2):
                out = out + rs_in[u, i, :, lanes].astype(F32)
            return out

        g, up = whole(0, 512), whole(512, 512)
        act[u, x, :, pl.ds(0, 512)] = (g / (1.0 + jnp.exp(-g)) * up).astype(BF)
        g = whole(1024, 128)
        up = pltpu.roll(g, 64, 1)
        lane = lax.broadcasted_iota(jnp.int32, (B, 128), 1)
        both = g / (1.0 + jnp.exp(-g)) * up
        act[u, x, :, pl.ds(512, 128)] = jnp.where(lane < 64, both, 0.0).astype(BF)
        gather_x(u, 1).start()
        gather_x(u, 3).start()

    def relay_act(u):
        for way in range(2):
            gather_x(u, 1 + 2 * way).wait_recv()
            relay_x(u, way).start()

    def project(u):
        for way in range(2):
            relay_x(u, way).wait_recv()
        a = act[u].reshape(CH, AW)
        for n in range(0, HW, 256):
            out = dot(a, wdn[1 - c, :, pl.ds(n, 256)]).astype(BF)
            d_send[u, :, :, pl.ds(n, 256)] = out.reshape(NY, B, 256)
        pair_down(u).start()
        for n in range(0, HW, 256):
            out = dot(a, wdn[c, :, pl.ds(n, 256)]).astype(BF)
            d_keep[u, :, :, pl.ds(n, 256)] = out.reshape(NY, B, 256)

    def pair(u):
        pair_down(u).wait_recv()
        for i in range(NY):
            both = d_keep[u, i].astype(F32) + d_in[u, i].astype(F32)
            d_keep[u, i] = both.astype(BF)
        for way in range(2):
            return_far(u, way).start()
        for way in range(2):
            return_near(u, way).start()

    def fold(u):
        for way in range(2):
            d, lanes = 1 + 2 * way, pl.ds(*ROW_WAYS[way])
            return_far(u, way).wait_recv()
            both = d_keep[u, d, :, lanes].astype(F32) + y_in[u, 0, :, lanes].astype(F32)
            d_keep[u, d, :, lanes] = both.astype(BF)
            return_both(u, way).start()

    def give(u):
        for way in range(2):
            return_near(u, way).wait_recv()
            return_both(u, way).wait_recv()
        whole = d_keep[u, 0].astype(F32)
        for i in (1, 2):
            whole = whole + y_in[u, i].astype(F32)
        whole = whole.astype(BF)

        @pl.when(u == 0)
        def _():
            z_ret[0] = whole

        @pl.when(u > 0)
        def _():
            z_send[u] = whole
            return_z(u).start()

    def lead(t):
        pass_y(t + 1)
        take_z(t + 2)

    end = NC - 1
    stages = [
        (give, 7, 0, end), (fold, 6, 0, end), (pair, 5, 0, end), (project, 4, 0, end),
        (relay_act, 3, 0, end), (activate, 2, 0, end), (reduce, 1, 0, end), (expand, 0, 0, end),
        (lead, 0, 0, 0), (pass_core, -1, 1, end), (pass_y, -2, 2, end), (take_z, -3, 3, end),
    ]

    def step(t, carry):
        for stage, lag, first, last in stages:

            @pl.when((t - lag >= first) & (t - lag <= last))
            def _(stage=stage, lag=lag):
                stage(t - lag)

        return carry

    lax.fori_loop(0, NC + 7, step, 0)

    total = jnp.zeros((2 * T, HW), F32)
    for t in range(NC):
        e = (z + NZ - DZ[t]) % NZ
        pick = jnp.where(slot == code[pl.ds(e, 1), :], gate[pl.ds(e, 1), :], 0.0)
        high = pick.astype(BF)
        low = (pick - high.astype(F32)).astype(BF)
        if t:
            return_z(t).wait_recv()
        rows = z_ret[t]
        total = total + dot(high, rows, ((0,), (0,))) + dot(low, rows, ((0,), (0,)))
    m_out[0] = total[:T]
    m_out[1] = total[T:]
    mix_copy = rcopy(m_out.at[1 - c], m_in, os_.at[0], or_.at[0], sib)
    mix_copy.start()
    lanes = pl.ds(pl.multiple_of(c * HW, HW), HW)
    mix[:, lanes] = (att[:, lanes].astype(F32) + m_out[c]).astype(BF)
    mix_copy.wait_recv()
    lanes = pl.ds(pl.multiple_of((1 - c) * HW, HW), HW)
    mix[:, lanes] = (att[:, lanes].astype(F32) + m_in[...]).astype(BF)

    meta_copy.wait_send()
    half_copy.wait_send()
    mix_copy.wait_send()
    for d in range(1, NP):
        scan_one(d).wait_send()
        scan_one_total(d).wait_send()
        scan_three(d).wait_send()
    for d in range(1, NZ):
        scan_two(d).wait_send()
        scan_two_total(d).wait_send()
    for dc, dx in others:
        square(dc, dx).wait_send()

    def sent(t, carry):
        spread_y(t, 1).wait_send()
        spread_y(t, 3).wait_send()
        spread_core(t).wait_send()
        gather_x(t, 1).wait_send()
        gather_x(t, 3).wait_send()
        pair_down(t).wait_send()
        for way in range(2):
            relay_y(t, way).wait_send()
            reduce_far(t, way).wait_send()
            reduce_near(t, way).wait_send()
            reduce_both(t, way).wait_send()
            relay_x(t, way).wait_send()
            return_far(t, way).wait_send()
            return_near(t, way).wait_send()
            return_both(t, way).wait_send()

        @pl.when(t > 0)
        def _():
            landed_z(t).wait_send()
            return_z(t).wait_send()

        return carry

    lax.fori_loop(0, NC, sent, 0)


def hand_over(a, b, a_out, b_out):
    a_out[...] = a[...]
    b_out[...] = b[...]


def on_device(hid, q, k, v, ld, ids, gates, gw, uw, dw):
    vmem = pl.BlockSpec(memory_space=pltpu.VMEM)
    anywhere = pl.BlockSpec(memory_space=pl.ANY)
    sem = pltpu.SemaphoreType.DMA
    buffers = [
        ((NP, SL, DH), BF), ((NP, SL, DH), BF), ((16, DH), F32), ((NP, 16, DH), F32),
        ((NP, SL, DH), F32), ((SL, DH), BF), ((NZ, SL, DH), BF), ((16, DH), F32),
        ((NZ, 16, DH), F32), ((NP, SL, DH), BF), ((NP, SL, DH), BF),
        ((T, W), F32), ((T, W), BF), ((8, T), F32), ((2, NX, 8, T), F32),
        ((2, T, HW), BF), ((T, HW), BF), ((2, T, HW), BF), ((NZ, B, 2 * T), BF), ((16, T), F32), ((16, T), F32), ((8, 2 * T), F32), ((8, 2 * T), F32),
        ((NZ, B, HW), BF), ((2, NC, NY, B, HW), BF), ((2, GU, HW), BF), ((2, AW, HW), BF),
        ((NC, NX, B, GU), BF), ((NC, NX - 1, B, GU), BF),
        ((NC, NX, B, AW), BF), ((NC, NY, B, HW), BF), ((NC, NY, B, HW), BF), ((NC, NY, B, HW), BF),
        ((NC, 3, B, HW), BF), ((NC, B, HW), BF), ((NC, B, HW), BF),
        ((2, T, HW), F32), ((T, HW), F32),
    ]
    pairs = [
        (7,), (7,), (7,), (7,), (7,), (7,), (1,), (1,),
    ]
    sems = [sem(n) for n in pairs for _ in range(2)]
    one, four, six = sem((NC,)), sem((NC, 4)), sem((NC, 6))
    sems += [one, one, four, four, one, one, six, six, four, four, one, one, six, six]
    sems += [one, one, sem((1,)), sem((1,)), sem((10,))]
    shapes = (jax.ShapeDtypeStruct((T, W), BF), jax.ShapeDtypeStruct((T, W), BF))
    results = pl.pallas_call(
        kernel,
        out_shape=shapes,
        in_specs=[vmem] * 7 + [anywhere] * 3,
        out_specs=(vmem, vmem),
        scratch_shapes=[pltpu.VMEM(shape, kind) for shape, kind in buffers] + sems,
        compiler_params=pltpu.CompilerParams(
            collective_id=0, has_side_effects=True, vmem_limit_bytes=60 << 20
        ),
        name="layer",
    )(hid, q, k, v, ld.T, ids.T, gates.T, gw.T, uw.T, dw)
    return pl.pallas_call(
        hand_over,
        out_shape=shapes,
        in_specs=[vmem] * 2,
        out_specs=(vmem, vmem),
        name="results",
    )(*results)


def solution(mesh):
    placed = (
        P("seq", "head"),
        P("seq", "head"),
        P("seq", "head"),
        P("seq", "head"),
        P("seq", "head"),
        P("seq", None),
        P("seq", None),
        P("head", "seq"),
        P("head", "seq"),
        P("seq", "head"),
    )
    return jax.shard_map(
        on_device,
        mesh=mesh,
        in_specs=placed,
        out_specs=(P("seq", "head"), P("seq", "head")),
        check_vma=False,
    )
```

```python
import jax
import jax.numpy as jnp
from jax import lax
from jax.experimental import pallas as pl
from jax.experimental.pallas import tpu as pltpu
from jax.sharding import PartitionSpec as P

MESH = pl.DeviceIdType.MESH
BF = jnp.bfloat16
F32 = jnp.float32

NZ, NY, NX = 8, 4, 4
NP = 8
T = 128
W = 1536
HW = 768
NH = 12
DH = 128
SL = NH * 16
CAP = 40
B = 2 * CAP
CH = NY * B
NC = NZ
FFD = 576
GU = 2 * FFD
AW = 640
SCALE = DH**-0.5
SUM_WAYS = ((0, 640), (640, 512))
ACT_WAYS = ((384, 256), (0, 384))
ROW_WAYS = ((0, 384), (384, 384))
DZ = (0, 1, 6, 2, 5, 3, 4, 7)


def rcopy(src, dst, ss, rs, dev):
    return pltpu.make_async_remote_copy(
        src_ref=src, dst_ref=dst, send_sem=ss, recv_sem=rs, device_id=dev, device_id_type=MESH
    )


def dot(a, b, dims=((1,), (0,)), precision=None):
    return lax.dot_general(
        a, b, (dims, ((), ())), preferred_element_type=F32, precision=precision
    )


def kernel(
    hid, q, k, v, ldt, idt, gt, gw, uw, dw,
    att, mix,
    s_loc, s_in, tot, tot_in, pfx, z_out, z_in, zt_out, zt_in, i_out, i_in,
    intra, qd, sq_out, sq_in, n_half, a_chip, tokens, picks, meta, meta_in, code, gate,
    packed, xb, wgu, wdn, part, rs_in, act, d_send, d_keep, d_in, y_in, z_send, z_ret,
    m_out, m_in,
    e1s, e1r, t1s, t1r, e2s, e2r, t2s, t2r, e3s, e3r, sqs, sqr, hs, hr, ms, mr,
    zs, zr, ys, yr, bs, br, rss, rsr, ags, agr, ds, dr, fs, fr, zbs, zbr, os_, or_, wsem,
):
    s = lax.axis_index("seq")
    x = lax.axis_index("head")
    z = s // NP
    p = s % NP
    y = p // 2
    c = p % 2

    def plane(d):
        return (z * NP + (p + d) % NP, x)

    def zpeer(d):
        return (((z + d) % NZ) * NP + p, x)

    def ypeer(d):
        return (z * NP + ((y + d) % NY) * 2 + c, x)

    def xpeer(d):
        return (s, (x + d) % NX)

    def xcore(dc, dx):
        return (z * NP + y * 2 + (c + dc) % 2, (x + dx) % NX)

    sib = (z * NP + y * 2 + (1 - c), x)

    loads = []
    for h in range(2):
        half = pl.ds(h * HW, HW)
        loads.append((gw.at[pl.ds(0, 512), half], wgu.at[h, pl.ds(0, 512), :]))
        loads.append((uw.at[pl.ds(0, 512), half], wgu.at[h, pl.ds(512, 512), :]))
        loads.append((gw.at[pl.ds(512, 64), half], wgu.at[h, pl.ds(1024, 64), :]))
        loads.append((uw.at[pl.ds(512, 64), half], wgu.at[h, pl.ds(1088, 64), :]))
        loads.append((dw.at[:, half], wdn.at[h, pl.ds(0, FFD), :]))
    loads = [pltpu.make_async_copy(a, b, wsem.at[i]) for i, (a, b) in enumerate(loads)]
    for copy in loads:
        copy.start()

    barrier = pltpu.get_barrier_semaphore()
    for d in range(1, NP):
        pl.semaphore_signal(barrier, inc=1, device_id=plane(d), device_id_type=MESH)
    for d in range(1, NZ):
        pl.semaphore_signal(barrier, inc=1, device_id=zpeer(d), device_id_type=MESH)
    for d in range(1, NX):
        pl.semaphore_signal(barrier, inc=1, device_id=xpeer(d), device_id_type=MESH)
        pl.semaphore_signal(barrier, inc=1, device_id=xcore(1, d), device_id_type=MESH)

    row = lax.broadcasted_iota(jnp.int32, (T, T), 0)
    col = lax.broadcasted_iota(jnp.int32, (T, T), 1)
    causal = row >= col
    hi = lax.Precision.HIGHEST
    lower = causal.astype(F32)
    upper = (row <= col).astype(F32)
    meta[pl.ds(0, NH), :] = ldt[...]
    meta[pl.ds(NH, 2), :] = idt[...].astype(F32)
    meta[pl.ds(NH + 2, 2), :] = gt[...]
    cumul = dot(lower, meta[...], ((1,), (1,)), precision=hi)
    cumul_t = dot(meta[...], upper, precision=hi)
    total = dot(meta[...], jnp.ones((T, T), F32), precision=hi)
    tot[...] = total
    for h in range(NH):
        hd = pl.ds(h * DH, DH)
        keyed = k[:, hd].astype(F32) * jnp.exp(total[h : h + 1, :] - cumul[:, h : h + 1])
        state = dot(keyed.astype(BF), v[:, hd], ((0,), (0,))).astype(BF)
        for j in range(NP):
            s_loc[j, pl.ds(16 * h, 16), :] = state[16 * j : 16 * j + 16, :]

    pl.semaphore_wait(barrier, (NP - 1) + (NZ - 1) + 2 * (NX - 1))

    meta_copy = rcopy(meta, meta_in, ms.at[0], mr.at[0], sib)
    meta_copy.start()

    def scan_one(d):
        return rcopy(s_loc.at[(p + d) % NP], s_in.at[p], e1s.at[d - 1], e1r.at[d - 1], plane(d))

    def scan_one_total(d):
        return rcopy(tot, tot_in.at[p], t1s.at[d - 1], t1r.at[d - 1], plane(d))

    for d in range(1, NP):
        scan_one_total(d).start()
        scan_one(d).start()
    s_in[p] = s_loc[p]
    tot_in[p] = tot[...]

    for h in range(NH):
        hd = pl.ds(h * DH, DH)
        own = cumul[:, h : h + 1]
        spread = jnp.where(causal, own - cumul_t[h : h + 1, :], 0.0)
        scores = dot(q[:, hd], k[:, hd], ((1,), (1,))) * SCALE
        weights = jnp.where(causal, scores * jnp.exp(spread), 0.0).astype(BF)
        intra[:, hd] = dot(weights, v[:, hd])
        qd[:, hd] = (q[:, hd].astype(F32) * (SCALE * jnp.exp(own))).astype(BF)

    for d in range(1, NP):
        scan_one_total(d).wait_recv()
        scan_one(d).wait_recv()

    def heads(tile):
        return jnp.concatenate(
            [jnp.broadcast_to(tile[h : h + 1, :], (16, DH)) for h in range(NH)], axis=0
        )

    run = jnp.zeros((SL, DH), F32)
    for j in range(NP):
        pfx[j] = run
        run = heads(jnp.exp(tot_in[j])) * run + s_in[j].astype(F32)
    z_out[...] = run.astype(BF)
    zt_out[...] = sum(tot_in[j] for j in range(NP))

    def scan_two(d):
        return rcopy(z_out, z_in.at[z], e2s.at[d - 1], e2r.at[d - 1], zpeer(d))

    def scan_two_total(d):
        return rcopy(zt_out, zt_in.at[z], t2s.at[d - 1], t2r.at[d - 1], zpeer(d))

    farthest = (4, 3, 5, 2, 6, 1, 7)
    for d in farthest:
        scan_two(d).start()
    for d in farthest:
        scan_two_total(d).start()
    z_in[z] = z_out[...]
    zt_in[z] = zt_out[...]

    meta_copy.wait_recv()
    expert = lax.broadcasted_iota(jnp.int32, (8, T), 0).astype(F32)
    strict = (row < col).astype(BF)

    def routing(m):
        first, second = expert == m[12:13, :], expert == m[13:14, :]
        chosen = jnp.where(first, 1.0, 0.0) + jnp.where(second, 1.0, 0.0)
        rank = dot(chosen.astype(BF), strict)
        value = jnp.where(first, m[14:15, :], 0.0) + jnp.where(second, m[15:16, :], 0.0)
        return jnp.where(chosen > 0.5, rank, -1000.0), value

    rank, value = routing(meta[...])
    mine = pl.ds(pl.multiple_of(c * T, T), T)
    code[:, mine] = rank + (c * CAP).astype(F32)
    gate[:, mine] = value
    rank, value = routing(meta_in[...])
    other = pl.ds(pl.multiple_of((1 - c) * T, T), T)
    code[:, other] = rank + ((1 - c) * CAP).astype(F32)
    gate[:, other] = value

    slot = lax.broadcasted_iota(jnp.int32, (B, 2 * T), 0).astype(F32)
    for t in range(NC):
        e = (z + NZ - DZ[t]) % NZ
        picks[t] = (slot == code[pl.ds(e, 1), :]).astype(BF)
    for h in range(2):
        wdn[h, pl.ds(FFD, AW - FFD), :] = jnp.zeros((AW - FFD, HW), BF)

    for d in range(1, NZ):
        scan_two_total(d).wait_recv()
        scan_two(d).wait_recv()
    run = jnp.zeros((SL, DH), F32)
    for j in range(NZ):
        new = heads(jnp.exp(zt_in[j])) * run + z_in[j].astype(F32)
        run = jnp.where(j < z, new, run)

    def scan_three(d):
        return rcopy(i_out.at[(p + d) % NP], i_in.at[p], e3s.at[d - 1], e3r.at[d - 1], plane(d))

    before = jnp.zeros((16, DH), F32)
    for j in range(NP):
        i_out[j] = (pfx[j] + heads(jnp.exp(before)) * run).astype(BF)
        before = before + tot_in[j]
    for d in range(1, NP):
        scan_three(d).start()
    i_in[p] = i_out[p]
    for d in range(1, NP):
        scan_three(d).wait_recv()

    squares = jnp.zeros((T, DH), F32)
    for h in range(NH):
        hd = pl.ds(h * DH, DH)
        state = jnp.concatenate([i_in[j, pl.ds(16 * h, 16), :] for j in range(NP)], axis=0)
        o = intra[:, hd] + dot(qd[:, hd], state)
        o = o * lax.rsqrt(jnp.mean(o * o, axis=1, keepdims=True) + 1e-05)
        a = (hid[:, hd].astype(F32) + o).astype(BF)
        att[:, hd] = a
        n_half[h // 6, :, pl.ds(DH * (h % 6), DH)] = a
        a = a.astype(F32)
        squares = squares + a * a
    half_copy = rcopy(n_half.at[1 - c], a_chip, hs.at[0], hr.at[0], sib)
    half_copy.start()

    sq_out[...] = dot(jnp.ones((8, T), F32), squares, ((1,), (1,)), precision=hi)
    others = [(dc, dx) for dc in range(2) for dx in range(NX) if dc or dx]

    def square(dc, dx):
        i = NX * dc + dx - 1
        return rcopy(sq_out, sq_in.at[c, x], sqs.at[i], sqr.at[i], xcore(dc, dx))

    for dc, dx in others:
        square(dc, dx).start()
    sq_in[c, x] = sq_out[...]
    for dc, dx in others:
        square(dc, dx).wait_recv()

    def normed(core, rows):
        whole = sum(sq_in[core, i] for i in range(NX))
        scale = lax.rsqrt(whole / (W * NX) + 1e-06).T[:, 0:1]
        return (rows.astype(F32) * scale).astype(BF)

    tokens[c] = normed(c, n_half[c])
    half_copy.wait_recv()
    tokens[1 - c] = normed(1 - c, a_chip[...])

    def dispatch(t):
        return rcopy(packed.at[t], xb.at[c, t, 0], zs.at[t], zr.at[t], zpeer(NZ - DZ[t]))

    def distance(t):
        return (1 - t % 2) * ((7 - t // 2) % 7) + (t % 2) * (1 + t // 2 + 3 * (t // 7))

    def landed_z(t):
        return rcopy(xb.at[c, t, 0], xb.at[c, t, 0], zs.at[t], zr.at[t], zpeer(1))

    def spread_y(t, d):
        i = d // 2
        return rcopy(xb.at[c, t, 0], xb.at[c, t, NY - d], ys.at[t, i], yr.at[t, i], ypeer(d))

    def relay_y(t, way):
        d, lanes = 1 + 2 * way, pl.ds(*ROW_WAYS[way])
        return rcopy(
            xb.at[c, t, NY - d, :, lanes], xb.at[c, t, 2, :, lanes],
            ys.at[t, 2 + way], yr.at[t, 2 + way], ypeer(d),
        )

    def pass_y(t):
        for way in range(2):
            spread_y(t, 1 + 2 * way).wait_recv()
            relay_y(t, way).start()

    def take_z(t):
        landed_z(t).wait_recv()
        spread_y(t, 1).start()
        spread_y(t, 3).start()

    def spread_core(t):
        return rcopy(xb.at[c, t], xb.at[c, t], bs.at[t], br.at[t], sib)

    def landed_core(t):
        return rcopy(xb.at[1 - c, t], xb.at[1 - c, t], bs.at[t], br.at[t], sib)

    def pass_core(t):
        for way in range(2):
            relay_y(t, way).wait_recv()
        spread_core(t).start()

    def sum_x(t, way, d, at, kind):
        lanes = pl.ds(*SUM_WAYS[way])
        i = 2 * kind + way
        return rcopy(
            part.at[t, at, :, lanes], rs_in.at[t, kind, :, lanes], rss.at[t, i], rsr.at[t, i], xpeer(d)
        )

    def reduce_far(t, way):
        return sum_x(t, way, 1 + 2 * way, (x + 2) % NX, 0)

    def reduce_near(t, way):
        return sum_x(t, way, 3 - 2 * way, (x + 3 - 2 * way) % NX, 1)

    def reduce_both(t, way):
        return sum_x(t, way, 1 + 2 * way, (x + 1 + 2 * way) % NX, 2)

    def gather_x(t, d):
        mine = act.at[t, x]
        return rcopy(mine, mine, ags.at[t, d // 2], agr.at[t, d // 2], xpeer(d))

    def relay_x(t, way):
        d = 1 + 2 * way
        there = act.at[t, (x + NX - d) % NX, :, pl.ds(*ACT_WAYS[way])]
        return rcopy(there, there, ags.at[t, 2 + way], agr.at[t, 2 + way], xpeer(d))

    def pair_down(t):
        return rcopy(d_send.at[t], d_in.at[t], ds.at[t], dr.at[t], sib)

    def sum_y(t, way, d, at, kind):
        lanes = pl.ds(*ROW_WAYS[way])
        i = 2 * kind + way
        return rcopy(
            d_keep.at[t, at, :, lanes], y_in.at[t, kind, :, lanes], fs.at[t, i], fr.at[t, i], ypeer(d)
        )

    def return_far(t, way):
        return sum_y(t, way, 1 + 2 * way, 2, 0)

    def return_near(t, way):
        return sum_y(t, way, 3 - 2 * way, 3 - 2 * way, 1)

    def return_both(t, way):
        return sum_y(t, way, 1 + 2 * way, 1 + 2 * way, 2)

    def return_z(t):
        return rcopy(z_send.at[t], z_ret.at[t], zbs.at[t], zbr.at[t], zpeer(distance(t)))

    chip = tokens[...].reshape(2 * T, HW)
    for t in range(NC):
        rows = dot(picks[t], chip).astype(BF)
        if t:
            packed[t] = rows
            dispatch(t).start()
        else:
            xb[c, 0, 0] = rows
            spread_y(0, 1).start()
            spread_y(0, 3).start()
    for copy in loads:
        copy.wait()
    pass_y(0)
    take_z(1)
    pass_core(0)

    cuts = [(n, min(256, GU - n)) for n in range(0, GU, 256)]

    def expand(t):
        landed_core(t).wait_recv()
        own, other = xb[c, t].reshape(CH, HW), xb[1 - c, t].reshape(CH, HW)
        for n, w in cuts:
            out = dot(own, wgu[c, pl.ds(n, w), :], ((1,), (1,)))
            out = out + dot(other, wgu[1 - c, pl.ds(n, w), :], ((1,), (1,)))
            out = out.astype(BF)
            for i in range(NX):
                part[t, i, :, pl.ds(n, w)] = out[B * i : B * i + B, :]
        for way in range(2):
            reduce_far(t, way).start()
        for way in range(2):
            reduce_near(t, way).start()

    def reduce(u):
        for way in range(2):
            there, lanes = (x + 1 + 2 * way) % NX, pl.ds(*SUM_WAYS[way])
            reduce_far(u, way).wait_recv()
            both = part[u, there, :, lanes].astype(F32) + rs_in[u, 0, :, lanes].astype(F32)
            part[u, there, :, lanes] = both.astype(BF)
            reduce_both(u, way).start()

    def activate(u):
        for way in range(2):
            reduce_near(u, way).wait_recv()
            reduce_both(u, way).wait_recv()

        def whole(n, w):
            lanes = pl.ds(n, w)
            out = part[u, x, :, lanes].astype(F32)
            for i in (1, 2):
                out = out + rs_in[u, i, :, lanes].astype(F32)
            return out

        g, up = whole(0, 512), whole(512, 512)
        act[u, x, :, pl.ds(0, 512)] = (g / (1.0 + jnp.exp(-g)) * up).astype(BF)
        g = whole(1024, 128)
        up = pltpu.roll(g, 64, 1)
        lane = lax.broadcasted_iota(jnp.int32, (B, 128), 1)
        both = g / (1.0 + jnp.exp(-g)) * up
        act[u, x, :, pl.ds(512, 128)] = jnp.where(lane < 64, both, 0.0).astype(BF)
        gather_x(u, 1).start()
        gather_x(u, 3).start()

    def relay_act(u):
        for way in range(2):
            gather_x(u, 1 + 2 * way).wait_recv()
            relay_x(u, way).start()

    def project(u):
        for way in range(2):
            relay_x(u, way).wait_recv()
        a = act[u].reshape(CH, AW)
        for n in range(0, HW, 256):
            out = dot(a, wdn[1 - c, :, pl.ds(n, 256)]).astype(BF)
            d_send[u, :, :, pl.ds(n, 256)] = out.reshape(NY, B, 256)
        pair_down(u).start()
        for n in range(0, HW, 256):
            out = dot(a, wdn[c, :, pl.ds(n, 256)]).astype(BF)
            d_keep[u, :, :, pl.ds(n, 256)] = out.reshape(NY, B, 256)

    def pair(u):
        pair_down(u).wait_recv()
        for i in range(NY):
            both = d_keep[u, i].astype(F32) + d_in[u, i].astype(F32)
            d_keep[u, i] = both.astype(BF)
        for way in range(2):
            return_far(u, way).start()
        for way in range(2):
            return_near(u, way).start()

    def fold(u):
        for way in range(2):
            d, lanes = 1 + 2 * way, pl.ds(*ROW_WAYS[way])
            return_far(u, way).wait_recv()
            both = d_keep[u, d, :, lanes].astype(F32) + y_in[u, 0, :, lanes].astype(F32)
            d_keep[u, d, :, lanes] = both.astype(BF)
            return_both(u, way).start()

    def give(u):
        for way in range(2):
            return_near(u, way).wait_recv()
            return_both(u, way).wait_recv()
        whole = d_keep[u, 0].astype(F32)
        for i in (1, 2):
            whole = whole + y_in[u, i].astype(F32)
        whole = whole.astype(BF)

        @pl.when(u == 0)
        def _():
            z_ret[0] = whole

        @pl.when(u > 0)
        def _():
            z_send[u] = whole
            return_z(u).start()

    def lead(t):
        pass_y(t + 1)
        take_z(t + 2)

    end = NC - 1
    stages = [
        (give, 7, 0, end), (fold, 6, 0, end), (pair, 5, 0, end), (project, 4, 0, end),
        (relay_act, 3, 0, end), (activate, 2, 0, end), (reduce, 1, 0, end), (expand, 0, 0, end),
        (lead, 0, 0, 0), (pass_core, -1, 1, end), (pass_y, -2, 2, end), (take_z, -3, 3, end),
    ]

    def step(t, carry):
        for stage, lag, first, last in stages:

            @pl.when((t - lag >= first) & (t - lag <= last))
            def _(stage=stage, lag=lag):
                stage(t - lag)

        return carry

    lax.fori_loop(0, NC + 7, step, 0)

    total = jnp.zeros((2 * T, HW), F32)
    for t in range(NC):
        e = (z + NZ - DZ[t]) % NZ
        pick = jnp.where(slot == code[pl.ds(e, 1), :], gate[pl.ds(e, 1), :], 0.0)
        high = pick.astype(BF)
        low = (pick - high.astype(F32)).astype(BF)
        if t:
            return_z(t).wait_recv()
        rows = z_ret[t]
        total = total + dot(high, rows, ((0,), (0,))) + dot(low, rows, ((0,), (0,)))
    m_out[0] = total[:T]
    m_out[1] = total[T:]
    mix_copy = rcopy(m_out.at[1 - c], m_in, os_.at[0], or_.at[0], sib)
    mix_copy.start()
    lanes = pl.ds(pl.multiple_of(c * HW, HW), HW)
    mix[:, lanes] = (att[:, lanes].astype(F32) + m_out[c]).astype(BF)
    mix_copy.wait_recv()
    lanes = pl.ds(pl.multiple_of((1 - c) * HW, HW), HW)
    mix[:, lanes] = (att[:, lanes].astype(F32) + m_in[...]).astype(BF)

    meta_copy.wait_send()
    half_copy.wait_send()
    mix_copy.wait_send()
    for d in range(1, NP):
        scan_one(d).wait_send()
        scan_one_total(d).wait_send()
        scan_three(d).wait_send()
    for d in range(1, NZ):
        scan_two(d).wait_send()
        scan_two_total(d).wait_send()
    for dc, dx in others:
        square(dc, dx).wait_send()

    def sent(t, carry):
        spread_y(t, 1).wait_send()
        spread_y(t, 3).wait_send()
        spread_core(t).wait_send()
        gather_x(t, 1).wait_send()
        gather_x(t, 3).wait_send()
        pair_down(t).wait_send()
        for way in range(2):
            relay_y(t, way).wait_send()
            reduce_far(t, way).wait_send()
            reduce_near(t, way).wait_send()
            reduce_both(t, way).wait_send()
            relay_x(t, way).wait_send()
            return_far(t, way).wait_send()
            return_near(t, way).wait_send()
            return_both(t, way).wait_send()

        @pl.when(t > 0)
        def _():
            landed_z(t).wait_send()
            return_z(t).wait_send()

        return carry

    lax.fori_loop(0, NC, sent, 0)


def hand_over(a, b, a_out, b_out):
    a_out[...] = a[...]
    b_out[...] = b[...]


def on_device(hid, q, k, v, ld, ids, gates, gw, uw, dw):
    vmem = pl.BlockSpec(memory_space=pltpu.VMEM)
    anywhere = pl.BlockSpec(memory_space=pl.ANY)
    sem = pltpu.SemaphoreType.DMA
    buffers = [
        ((NP, SL, DH), BF), ((NP, SL, DH), BF), ((16, DH), F32), ((NP, 16, DH), F32),
        ((NP, SL, DH), F32), ((SL, DH), BF), ((NZ, SL, DH), BF), ((16, DH), F32),
        ((NZ, 16, DH), F32), ((NP, SL, DH), BF), ((NP, SL, DH), BF),
        ((T, W), F32), ((T, W), BF), ((8, T), F32), ((2, NX, 8, T), F32),
        ((2, T, HW), BF), ((T, HW), BF), ((2, T, HW), BF), ((NZ, B, 2 * T), BF), ((16, T), F32), ((16, T), F32), ((8, 2 * T), F32), ((8, 2 * T), F32),
        ((NZ, B, HW), BF), ((2, NC, NY, B, HW), BF), ((2, GU, HW), BF), ((2, AW, HW), BF),
        ((NC, NX, B, GU), BF), ((NC, NX - 1, B, GU), BF),
        ((NC, NX, B, AW), BF), ((NC, NY, B, HW), BF), ((NC, NY, B, HW), BF), ((NC, NY, B, HW), BF),
        ((NC, 3, B, HW), BF), ((NC, B, HW), BF), ((NC, B, HW), BF),
        ((2, T, HW), F32), ((T, HW), F32),
    ]
    pairs = [
        (7,), (7,), (7,), (7,), (7,), (7,), (1,), (1,),
    ]
    sems = [sem(n) for n in pairs for _ in range(2)]
    one, four, six = sem((NC,)), sem((NC, 4)), sem((NC, 6))
    sems += [one, one, four, four, one, one, six, six, four, four, one, one, six, six]
    sems += [one, one, sem((1,)), sem((1,)), sem((10,))]
    shapes = (jax.ShapeDtypeStruct((T, W), BF), jax.ShapeDtypeStruct((T, W), BF))
    results = pl.pallas_call(
        kernel,
        out_shape=shapes,
        in_specs=[vmem] * 7 + [anywhere] * 3,
        out_specs=(vmem, vmem),
        scratch_shapes=[pltpu.VMEM(shape, kind) for shape, kind in buffers] + sems,
        compiler_params=pltpu.CompilerParams(
            collective_id=0, has_side_effects=True, vmem_limit_bytes=60 << 20
        ),
        name="layer",
    )(hid, q, k, v, ld.T, ids.T, gates.T, gw.T, uw.T, dw)
    return pl.pallas_call(
        hand_over,
        out_shape=shapes,
        in_specs=[vmem] * 2,
        out_specs=(vmem, vmem),
        name="results",
    )(*results)


def solution(mesh):
    placed = (
        P("seq", "head"),
        P("seq", "head"),
        P("seq", "head"),
        P("seq", "head"),
        P("seq", "head"),
        P("seq", None),
        P("seq", None),
        P("head", "seq"),
        P("head", "seq"),
        P("seq", "head"),
    )
    return jax.shard_map(
        on_device,
        mesh=mesh,
        in_specs=placed,
        out_specs=(P("seq", "head"), P("seq", "head")),
        check_vma=False,
    )
```
